128 devices in a mesh: blk: 16 (over z, x_hi, core), grp: 8 (over x_lo, y).
Axes of the slice: x: 4 (x_hi: 2, x_lo: 2; x = x_hi * 2 + x_lo), y: 4, z: 4, core: 2. Of those that a mesh axis runs over, the one named last changes fastest.
Arguments:
- queries: bfloat16 [4096, 3584], P(('blk', 'grp')), may hold values from -8 to 8
- stored_documents: bfloat16 [16384, 3584], P('blk'), may hold values from -8 to 8
- positive: int32 [4096], P(('blk', 'grp')), may hold values from 0 to 16383, as said below
- last_hidden: bfloat16 [256, 3584], P(('blk', 'grp')), may hold values from -150 to 150
- norm_gain: float32 [3584], replicated, may hold values from 0.1 to 1.9
- gate_weight: bfloat16 [3584, 18944], P('grp', 'blk'), may hold values from -0.09375 to 0.09375
- up_weight: bfloat16 [3584, 18944], P('grp', 'blk'), may hold values from -0.09375 to 0.09375
- down_weight: bfloat16 [18944, 3584], P('blk', 'grp'), may hold values from -0.046875 to 0.046875
Outputs:
- losses: float32 [4096], P(('blk', 'grp'))
- passage_grads: float32 [16384, 3584], P(('blk', 'grp'))
- hidden_grads: float32 [256, 3584], P(('blk', 'grp'))
The draws below stay inside these ranges and needn't reach their ends.
Inputs may be any that keep to these rules, and one draw needn't show every extreme that they name: No two queries share a positive passage.
All inputs are finite; a program needn't handle non-finite values.
Results may differ from the reference program's by a relative error of at most 0.019.
Values may be sent and summed in bfloat16 or wider, within the bound.
No kernel may reach another device: no remote copies, remote signals or barrier semaphores. Data moves between devices by JAX's collectives and lax.ppermute only.
A program may use at most 128 MiB of HBM per device.

```python
import math
import jax
import jax.numpy as jnp
from jax import lax

D = 3584
FF = 18944
QC = 32
PC = 1024
SUB_DEV = 2
B = 4096
NP = 16384
S = 256
N_BLK = 16
N_GRP = 8


def draw_stored_documents(key, part):
    key_entry, key_scale = jax.random.split(jax.random.fold_in(key, 13), 2)
    unit_scale = 1.0 / math.sqrt(D)
    row_index = jnp.arange(NP, dtype=jnp.float32)[:, None]
    entries = jax.random.truncated_normal(key_entry, -6.0, 6.0, (NP, D), jnp.float32)
    spread = jnp.exp(jax.random.uniform(key_scale, (NP, 1), jnp.float32, math.log(0.3), math.log(3.0)))
    rising = 0.6 + 1.2 * row_index / NP
    matrix = entries * spread * rising * unit_scale
    return matrix.astype(jnp.bfloat16)


def draw_queries(key, part):
    key_entry, key_scale = jax.random.split(jax.random.fold_in(key, 29), 2)
    unit_scale = 1.0 / math.sqrt(D)
    entries = jax.random.truncated_normal(key_entry, -6.0, 6.0, (B, D), jnp.float32)
    spread = jnp.exp(jax.random.uniform(key_scale, (B, 1), jnp.float32, math.log(0.5), math.log(1.5)))
    matrix = entries * spread * unit_scale
    return matrix.astype(jnp.bfloat16)


def draw_positive(key, part):
    shuffled = jax.random.permutation(jax.random.fold_in(key, 5), B).astype(jnp.int32)
    stride = NP // B
    return (shuffled * stride + shuffled % stride).astype(jnp.int32)


def draw_last_hidden(key, part):
    key_entry, key_rows, key_cols = jax.random.split(jax.random.fold_in(key, 41), 3)
    column_scale = jnp.exp(jax.random.uniform(key_cols, (1, D), jnp.float32, math.log(0.5), math.log(2.0)))
    entries = jax.random.truncated_normal(key_entry, -6.0, 6.0, (S, D), jnp.float32)
    row_multiplier = jnp.exp(jax.random.uniform(key_rows, (S, 1), jnp.float32, math.log(1.0), math.log(10.0)))
    matrix = entries * row_multiplier * column_scale
    return matrix.astype(jnp.bfloat16)


def block_scale(rng, shape, pieces, least, top_value):
    loudness, own = 1.0, jax.random.fold_in(rng, 6)
    for axis_at, parts in pieces:
        steps = jnp.exp(jax.random.uniform(jax.random.fold_in(own, axis_at), (parts,), jnp.float32, least / len(pieces), top_value / len(pieces)))
        loudness = loudness * jnp.repeat(steps, shape[axis_at] // parts).reshape([-1 if axis == axis_at else 1 for axis in range(len(shape))])
    return loudness


def gaussian(stream_key, dims, width, most, pieces=(), held_as=jnp.bfloat16):
    values = width * jax.random.normal(stream_key, dims, jnp.float32)
    if pieces:
        values = values * block_scale(stream_key, dims, pieces, -0.22, 0.18)
    return jnp.clip(values, -most, most).astype(held_as)


def setup_inputs(seed: int = 0) -> dict:
    keys = jax.random.split(jax.random.key(seed), 9)
    return {
        "queries": draw_queries(jax.random.fold_in(keys[8], 71), 0),
        "stored_documents": draw_stored_documents(jax.random.fold_in(keys[8], 71), 0),
        "positive": draw_positive(jax.random.fold_in(keys[8], 71), 0),
        "last_hidden": draw_last_hidden(jax.random.fold_in(keys[8], 71), 0),
        "norm_gain": jnp.clip(1.0 + 0.18 * jax.random.normal(keys[4], (D,), jnp.float32), 0.1, 1.9),
        "gate_weight": gaussian(keys[5], (D, FF), D ** -0.5, 0.09375, ((0, 8), (1, 16))),
        "up_weight": gaussian(keys[6], (D, FF), D ** -0.5, 0.09375, ((0, 8), (1, 16))),
        "down_weight": gaussian(keys[7], (FF, D), FF ** -0.5, 0.046875, ((0, 16), (1, 8))),
    }


sharpness_scale = 20.0
epsilon = 1e-06

def matmul(left_side, right_side):
    return jnp.dot(left_side.astype(jnp.float32), right_side.astype(jnp.float32), preferred_element_type=jnp.float32)

def rounded(matrix):
    return lax.optimization_barrier(matrix.astype(jnp.bfloat16)).astype(jnp.float32)

def reference(queries, stored_documents, positive, last_hidden, norm_gain, gate_weight, up_weight, down_weight):
    document_vectors_wide = stored_documents.astype(jnp.float32)
    document_subsets = document_vectors_wide.reshape(N_BLK, PC, D)
    query_lattice = queries.reshape(N_BLK, N_GRP, QC, D)
    pos_grid = positive.reshape(N_BLK, N_GRP, QC)
    column_ids = jnp.arange(NP, dtype=jnp.int32)
    passage_grads = jnp.zeros((NP, D), jnp.float32)
    loss_parts = []
    grad_parts = []
    for column in range(N_GRP):
        search_texts_across = query_lattice[:, column].reshape(N_BLK * QC, D).astype(jnp.float32)
        column_pos = pos_grid[:, column].reshape(N_BLK * QC)
        similarity_scores = sharpness_scale * jnp.dot(search_texts_across, document_vectors_wide.T, preferred_element_type=jnp.float32)
        highest = lax.optimization_barrier(jnp.max(similarity_scores, axis=1, keepdims=True))
        log_total = highest + jnp.log(lax.optimization_barrier(jnp.sum(jnp.exp(similarity_scores - highest), axis=1, keepdims=True)))
        onehot = (column_ids[None, :] == column_pos[:, None]).astype(jnp.float32)
        pos_logit = lax.optimization_barrier(jnp.sum(similarity_scores * onehot, axis=1))
        loss_parts.append((log_total[:, 0] - pos_logit).reshape(N_BLK, 1, QC))
        layer_parameters = rounded(jnp.exp(similarity_scores - log_total) - onehot)
        subset_coefficients = layer_parameters.reshape(N_BLK * QC, N_BLK, PC)
        linear_branch_ratio = sharpness_scale * jnp.einsum('zcn,cnk->czk', subset_coefficients, document_subsets)
        column_grads = lax.optimization_barrier(jnp.sum(rounded(linear_branch_ratio), axis=0))
        grad_parts.append(column_grads.reshape(N_BLK, 1, QC, D))
        document_contribution = sharpness_scale * jnp.dot(layer_parameters.T, search_texts_across, preferred_element_type=jnp.float32)
        passage_grads = passage_grads + rounded(document_contribution)
    losses = jnp.concatenate(loss_parts, axis=1).reshape(N_BLK * N_GRP * QC)
    query_grads = jnp.concatenate(grad_parts, axis=1).reshape(N_BLK * N_GRP, QC, D)
    cotangent = query_grads[:, :SUB_DEV].reshape(S, D).astype(jnp.bfloat16)
    hidden_f = last_hidden.astype(jnp.float32)
    inv_rms = lax.rsqrt(lax.optimization_barrier(jnp.mean(hidden_f * hidden_f, axis=1, keepdims=True)) + epsilon)
    gain_row = norm_gain.astype(jnp.float32)
    normed = (hidden_f * inv_rms * gain_row).astype(jnp.bfloat16)
    gate_value = matmul(normed, gate_weight)
    up_value = matmul(normed, up_weight)
    gate_sigmoid = jax.nn.sigmoid(gate_value)
    act_grad = matmul(cotangent, down_weight.T)
    up_grad = (act_grad * gate_value * gate_sigmoid).astype(jnp.bfloat16)
    gate_grad = (act_grad * up_value * gate_sigmoid * (1.0 + gate_value * (1.0 - gate_sigmoid))).astype(jnp.bfloat16)
    normed_grad = matmul(gate_grad, gate_weight.T) + matmul(up_grad, up_weight.T)
    scaled = normed_grad * gain_row
    hidden_grads = cotangent.astype(jnp.float32) + inv_rms * scaled - hidden_f * inv_rms * inv_rms * inv_rms * lax.optimization_barrier(jnp.mean(hidden_f * scaled, axis=1, keepdims=True))
    return (losses, passage_grads, hidden_grads)
```

```python
import functools

import jax
import jax.numpy as jnp
from jax import lax
from jax.experimental import pallas as pl
from jax.experimental.pallas import tpu as pltpu
from jax.sharding import PartitionSpec as P

sharpness_scale = 20.0
epsilon = 1e-06
contract_last = (((1,), (1,)), ((), ()))
Z, X, C = 4, 2, 2
N_BLK, N_GRP = 16, 8
POS_LANES = 128
POS_BASE = 128
BIG_VMEM = 56 * 1024 * 1024


def blk_shift(dz, dx, dc):
    pairs = []
    for s in range(N_BLK):
        z, x, c = s // (X * C), s // C % X, s % C
        pairs.append((s, ((z + dz) % Z * X + (x + dx) % X) * C + (c + dc) % C))
    return pairs


def whole(shape):
    return pl.BlockSpec(shape, lambda *_: (0,) * len(shape))


def vmem(count):
    return [pl.BlockSpec(memory_space=pltpu.VMEM)] * count


def gather_column(block):
    send = lambda v, *shift: lax.ppermute(v, "blk", blk_shift(*shift))
    half = block.shape[0] // 2
    below = send(block, 1, 0, 0)
    above = send(block, -1, 0, 0)
    across = send(block, 0, 1, 0)
    across_below = send(across, 1, 0, 0)
    far = send(above, -1, 0, 0)
    across_above = send(above, 0, 1, 0)
    across_far_a = send(across_below[:half], 1, 0, 0)
    across_far_b = send(far[half:], 0, 1, 0)
    own = [
        (block, 0, 0),
        (below, -1, 0),
        (above, 1, 0),
        (across, 0, 1),
        (across_below, -1, 1),
        (far, 2, 0),
        (across_above, 1, 1),
        (across_far_a, 2, 1),
        (across_far_b, 2, 1),
    ]
    pieces = [(v, dz, dx, 0) for v, dz, dx in own]
    pieces += [(send(v, 0, 0, 1), dz, dx, 1) for v, dz, dx in own]
    return pieces


def score_kernel(starts, tile, place_ref, *refs):
    n = len(starts)
    blocks, doc_ref = refs[:n], refs[n]
    score_ref, query_ref, stat_ref, pos_ref, pos_col = refs[n + 1 :]
    step = pl.program_id(0)
    dim = query_ref.shape[1]

    @pl.when(step == 0)
    def _():
        for k, block in enumerate(blocks):
            rows = block.shape[0]
            at = pl.multiple_of(place_ref[k], 16)
            query_ref[pl.ds(at, rows), :] = block[:, :dim]
            pos_col[pl.ds(at, rows), :] = block[:, dim:]
        lane = lax.broadcasted_iota(jnp.int32, (8, POS_LANES), 1)
        line = lax.broadcasted_iota(jnp.int32, (8, POS_LANES), 0)
        pick = jnp.where(lane == line, 1.0, 0.0).astype(jnp.bfloat16)
        parts = lax.dot_general(pick, pos_col[...], contract_last, preferred_element_type=jnp.float32)
        pos_ref[...] = (parts[0:1] * POS_BASE + parts[1:2]).astype(jnp.int32)
        stat_ref[...] = jnp.zeros_like(stat_ref)
        stat_ref[0:1] = jnp.full_like(stat_ref[0:1], -jnp.inf)

    scores = sharpness_scale * lax.dot_general(
        doc_ref[...], query_ref[...], contract_last, preferred_element_type=jnp.float32
    )
    score_ref[...] = scores
    top_before = stat_ref[0:1]
    top = jnp.maximum(top_before, jnp.max(scores, axis=0, keepdims=True))
    slot = place_ref[n] + step * tile + lax.broadcasted_iota(jnp.int32, scores.shape, 0)
    hit = jnp.where(slot == pos_ref[...], scores, 0.0)
    stat_ref[0:1] = top
    stat_ref[1:2] = stat_ref[1:2] * jnp.exp(top_before - top) + jnp.sum(
        jnp.exp(scores - top), axis=0, keepdims=True
    )
    stat_ref[2:3] = stat_ref[2:3] + jnp.sum(hit, axis=0, keepdims=True)


def column_scores(pieces, docs, row_places, first_passage, dim):
    shard_rows = docs.shape[0]
    cols = 512
    tile = 256
    places = jnp.concatenate([row_places, first_passage[None]])
    return pl.pallas_call(
        functools.partial(score_kernel, tuple(range(len(pieces))), tile),
        grid_spec=pltpu.PrefetchScalarGridSpec(
            num_scalar_prefetch=1,
            grid=(shard_rows // tile,),
            in_specs=[whole(v.shape) for v in pieces]
            + [pl.BlockSpec((tile, dim), lambda i, _: (i, 0))],
            out_specs=[
                pl.BlockSpec((tile, cols), lambda i, _: (i, 0)),
                whole((cols, dim)),
                whole((8, cols)),
                whole((1, cols)),
            ],
            scratch_shapes=[pltpu.VMEM((cols, POS_LANES), jnp.bfloat16)],
        ),
        out_shape=[
            jax.ShapeDtypeStruct((shard_rows, cols), jnp.float32),
            jax.ShapeDtypeStruct((cols, dim), jnp.bfloat16),
            jax.ShapeDtypeStruct((8, cols), jnp.float32),
            jax.ShapeDtypeStruct((1, cols), jnp.int32),
        ],
        compiler_params=pltpu.CompilerParams(vmem_limit_bytes=BIG_VMEM),
        cost_estimate=pl.CostEstimate(
            flops=2 * shard_rows * cols * dim,
            bytes_accessed=2 * (shard_rows + 2 * cols) * dim,
            transcendentals=shard_rows * cols,
        ),
        name="column_scores",
    )(places, *pieces, docs)


def weight_kernel(tile, rows, sub, first_ref, score_ref, stats_ref, pos_ref, doc_ref, weight_ref, grad_ref, loss_ref, total, acc):
    step = pl.program_id(0)
    cols = score_ref.shape[1]

    @pl.when(step == 0)
    def _():
        tops = stats_ref[:, 0, :]
        top = jnp.max(tops, axis=0, keepdims=True)
        summed = jnp.sum(stats_ref[:, 1, :] * jnp.exp(tops - top), axis=0, keepdims=True)
        total[...] = top + jnp.log(summed)
        loss_ref[...] = total[...] - jnp.sum(stats_ref[:, 2, :], axis=0, keepdims=True)
        acc[...] = jnp.zeros_like(acc)

    slot = first_ref[0] + step * tile + lax.broadcasted_iota(jnp.int32, score_ref.shape, 0)
    onehot = jnp.where(slot == pos_ref[...], 1.0, 0.0)
    weights = (jnp.exp(score_ref[...] - total[...]) - onehot).astype(jnp.bfloat16)
    weight_ref[...] = weights
    line = lax.broadcasted_iota(jnp.int32, (acc.shape[0], cols), 0)
    lane = lax.broadcasted_iota(jnp.int32, (acc.shape[0], cols), 1)
    pick = jnp.where(lane == line // sub * rows + line % sub, 1.0, 0.0).astype(jnp.bfloat16)
    picked = lax.dot_general(pick, weights, contract_last, preferred_element_type=jnp.float32).astype(jnp.bfloat16)
    acc[...] += jnp.dot(picked, doc_ref[...], preferred_element_type=jnp.float32)

    @pl.when(step == pl.num_programs(0) - 1)
    def _():
        grads = (sharpness_scale * acc[...]).astype(jnp.bfloat16)
        width = grad_ref.shape[2]
        for g in range(grad_ref.shape[0]):
            grad_ref[g] = grads[:, g * width : (g + 1) * width]


def column_weights(scores, stats, positives, docs, first_passage, rows, sub):
    shard_rows, cols = scores.shape
    dim = docs.shape[1]
    tile = 256
    lines = cols // rows * sub
    return pl.pallas_call(
        functools.partial(weight_kernel, tile, rows, sub),
        grid_spec=pltpu.PrefetchScalarGridSpec(
            num_scalar_prefetch=1,
            grid=(shard_rows // tile,),
            in_specs=[
                pl.BlockSpec((tile, cols), lambda i, _: (i, 0)),
                whole(stats.shape),
                whole((1, cols)),
                pl.BlockSpec((tile, dim), lambda i, _: (i, 0)),
            ],
            out_specs=[
                pl.BlockSpec((tile, cols), lambda i, _: (i, 0)),
                whole((N_GRP, lines, dim // N_GRP)),
                whole((1, cols)),
            ],
            scratch_shapes=[
                pltpu.VMEM((1, cols), jnp.float32),
                pltpu.VMEM((lines, dim), jnp.float32),
            ],
        ),
        out_shape=[
            jax.ShapeDtypeStruct((shard_rows, cols), jnp.bfloat16),
            jax.ShapeDtypeStruct((N_GRP, lines, dim // N_GRP), jnp.bfloat16),
            jax.ShapeDtypeStruct((1, cols), jnp.float32),
        ],
        compiler_params=pltpu.CompilerParams(vmem_limit_bytes=BIG_VMEM),
        cost_estimate=pl.CostEstimate(
            flops=2 * shard_rows * (cols + dim) * lines,
            bytes_accessed=2 * shard_rows * dim,
            transcendentals=shard_rows * cols,
        ),
        name="column_weights",
    )(first_passage[None], scores, stats, positives, docs)


def everyone(value, axis):
    size = N_BLK if axis == "blk" else N_GRP
    return lax.all_to_all(
        jnp.broadcast_to(value[None], (size, *value.shape)), axis, 0, 0, tiled=True
    )


def reduce_rows(partial):
    parts = partial.astype(jnp.bfloat16).reshape(N_GRP, -1, partial.shape[1])
    got = lax.all_to_all(parts, "grp", 0, 0, tiled=True)
    return jnp.sum(got.astype(jnp.float32), axis=0)


def shards(
    queries, stored_documents, positive, last_hidden, norm_gain, gate_weight, up_weight, down_weight
):
    blk_pos = lax.axis_index("blk")
    z, x, c = blk_pos // (X * C), blk_pos // C % X, blk_pos % C
    shard_rows, dim = stored_documents.shape
    own_rows = queries.shape[0]
    sub = last_hidden.shape[0]
    part = dim // N_GRP
    first_passage = blk_pos * shard_rows

    lane = lax.broadcasted_iota(jnp.int32, (own_rows, POS_LANES), 1)
    coded = jnp.where(
        lane == 0,
        (positive // POS_BASE)[:, None],
        jnp.where(lane == 1, (positive % POS_BASE)[:, None], 0),
    )
    block = jnp.concatenate([queries, coded.astype(jnp.bfloat16)], axis=1)
    pieces = gather_column(block)
    row_places = []
    seen = set()
    for _, dz, dx, dc in pieces:
        place = (((z + dz) % Z * X + (x + dx) % X) * C + (c + dc) % C) * own_rows
        row_places.append(place + (own_rows // 2 if (dz, dx, dc) in seen else 0))
        seen.add((dz, dx, dc))
    row_places = jnp.stack(row_places).astype(jnp.int32)
    scores, col_queries, stats, col_pos = column_scores(
        [v for v, *_ in pieces], stored_documents, row_places, first_passage, dim
    )

    hidden_f = last_hidden.astype(jnp.float32)
    inv_rms = lax.rsqrt(jnp.mean(hidden_f * hidden_f, axis=1, keepdims=True) + epsilon)
    normed = (hidden_f * inv_rms * norm_gain).astype(jnp.bfloat16)
    normed_parts = normed.reshape(sub, N_GRP, part).transpose(1, 0, 2)
    normed_cols = lax.all_to_all(
        jnp.broadcast_to(normed_parts[None], (N_BLK, N_GRP, sub, part)).reshape(-1, sub, part),
        ("blk", "grp"),
        0,
        0,
        tiled=True,
    ).reshape(-1, part)
    gate_part = jnp.dot(normed_cols, gate_weight, preferred_element_type=jnp.float32)
    up_part = jnp.dot(normed_cols, up_weight, preferred_element_type=jnp.float32)
    forward = reduce_rows(jnp.concatenate([gate_part, up_part], axis=1)).astype(jnp.bfloat16)
    hidden_units = gate_weight.shape[1]
    forward = everyone(forward, "grp").reshape(-1, 2 * hidden_units).astype(jnp.float32)
    gate_value, up_value = forward[:, :hidden_units], forward[:, hidden_units:]

    weights, sub_grads, loss_row = column_weights(
        scores, everyone(stats, "blk"), col_pos, stored_documents, first_passage, own_rows, sub
    )
    losses = lax.dynamic_slice_in_dim(loss_row[0], blk_pos * own_rows, own_rows)
    got = lax.all_to_all(
        sub_grads.reshape(N_GRP * N_BLK, sub, part), ("grp", "blk"), 0, 0, tiled=True
    )
    cot_rows = jnp.sum(got.reshape(N_GRP, N_BLK, sub, part).astype(jnp.float32), axis=1)
    cot_rows = cot_rows.astype(jnp.bfloat16)

    passage_part = (
        sharpness_scale * jnp.dot(weights, col_queries, preferred_element_type=jnp.float32)
    ).astype(jnp.bfloat16)
    passage_got = lax.all_to_all(
        passage_part.reshape(N_GRP, -1, dim), "grp", 0, 0, tiled=True
    )
    passage_grads = jnp.sum(passage_got.astype(jnp.float32), axis=0)

    cot_cols = everyone(cot_rows.reshape(-1, part), "blk").reshape(-1, part)
    act_part = lax.dot_general(
        cot_cols, down_weight, contract_last, preferred_element_type=jnp.float32
    )
    act_rows = reduce_rows(act_part).astype(jnp.bfloat16)
    act_grad = everyone(act_rows, "grp").reshape(-1, hidden_units).astype(jnp.float32)
    gate_sigmoid = jax.nn.sigmoid(gate_value)
    up_grad = (act_grad * gate_value * gate_sigmoid).astype(jnp.bfloat16)
    gate_grad = (
        act_grad * up_value * gate_sigmoid * (1.0 + gate_value * (1.0 - gate_sigmoid))
    ).astype(jnp.bfloat16)
    from_gate = lax.dot_general(
        gate_grad, gate_weight, contract_last, preferred_element_type=jnp.float32
    )
    from_up = lax.dot_general(up_grad, up_weight, contract_last, preferred_element_type=jnp.float32)
    normed_part = (from_gate + from_up).astype(jnp.bfloat16).reshape(N_BLK, N_GRP, sub, part)
    cot_sent = cot_cols.reshape(normed_part.shape)
    back = lax.all_to_all(
        jnp.concatenate([normed_part, cot_sent], axis=2).reshape(-1, 2 * sub, part),
        ("blk", "grp"),
        0,
        0,
        tiled=True,
    ).reshape(N_BLK, N_GRP, 2 * sub, part)
    normed_grad = jnp.sum(back[:, :, :sub].astype(jnp.float32), axis=0)
    normed_grad = normed_grad.transpose(1, 0, 2).reshape(sub, dim)
    cotangent = back[0, :, sub:].transpose(1, 0, 2).reshape(sub, dim).astype(jnp.float32)
    scaled = normed_grad * norm_gain
    hidden_grads = (
        cotangent
        + inv_rms * scaled
        - hidden_f
        * inv_rms
        * inv_rms
        * inv_rms
        * jnp.mean(hidden_f * scaled, axis=1, keepdims=True)
    )
    return (losses, passage_grads, hidden_grads)


def solution(mesh):
    return jax.shard_map(
        shards,
        mesh=mesh,
        in_specs=(
            P(("blk", "grp"), None),
            P("blk", None),
            P(("blk", "grp")),
            P(("blk", "grp"), None),
            P(),
            P("grp", "blk"),
            P("grp", "blk"),
            P("blk", "grp"),
        ),
        out_specs=(P(("blk", "grp")), P(("blk", "grp"), None), P(("blk", "grp"), None)),
        check_vma=False,
    )
```

```python
import functools

import jax
import jax.numpy as jnp
from jax import lax
from jax.experimental import pallas as pl
from jax.experimental.pallas import tpu as pltpu
from jax.sharding import PartitionSpec as P

sharpness_scale = 20.0
epsilon = 1e-06
contract_last = (((1,), (1,)), ((), ()))
Z, X, C = 4, 2, 2
N_BLK, N_GRP = 16, 8
POS_BASE = 128
TAIL = 128
ROWS = 32
SUB = 2
WIDE = 3 * SUB
LANES = 512
TILE = 256
f32, bf16 = jnp.float32, jnp.bfloat16
VMEM = pl.BlockSpec(memory_space=pltpu.VMEM)
SMEM = pl.BlockSpec(memory_space=pltpu.SMEM)


def local(kernel, name, out_shape, scratch=(), scalars=0, count=0, flops=0, moved=0, vmem=32):
    return pl.pallas_call(
        kernel,
        in_specs=[SMEM] * scalars + [VMEM] * count,
        out_specs=jax.tree.map(lambda _: VMEM, out_shape),
        out_shape=out_shape,
        scratch_shapes=list(scratch),
        compiler_params=pltpu.CompilerParams(vmem_limit_bytes=vmem * 1024 * 1024),
        cost_estimate=pl.CostEstimate(flops=flops, bytes_accessed=moved, transcendentals=0),
        name=name,
    )


def blk_shift(dz, dx, dc):
    pairs = []
    for s in range(N_BLK):
        z, x, c = s // (X * C), s // C % X, s % C
        pairs.append((s, ((z + dz) % Z * X + (x + dx) % X) * C + (c + dc) % C))
    return pairs


def send(v, *shift):
    return lax.ppermute(v, "blk", blk_shift(*shift))


def near_column(block):
    own = [block, send(block, 1, 0, 0), send(block, -1, 0, 0), send(block, 0, 1, 0)]
    return own + [send(v, 0, 0, 1) for v in own]


def far_column(below, above, across):
    across_below = send(across, 1, 0, 0)
    far = send(above, -1, 0, 0)
    across_above = send(above, 0, 1, 0)
    return across_below, far, across_above


def far_rest(across_below, far, across_above, half):
    own = [
        across_below,
        far,
        across_above,
        send(across_below[:half], 1, 0, 0),
        send(far[half:], 0, 1, 0),
    ]
    return own + [send(v, 0, 0, 1) for v in own]


def places_of(blk):
    z, x, c = blk // (X * C), blk // C % X, blk % C
    shifts = [(0, 0), (-1, 0), (1, 0), (0, 1)], [(-1, 1), (2, 0), (1, 1), (2, 1)]
    return [
        ((z + dz + Z) % Z * X + (x + dx) % X) * C + (c + dc) % C
        for batch in shifts
        for dc in range(C)
        for dz, dx in batch
    ]


def block_kernel(pos_ref, query_ref, out_ref):
    dim = query_ref.shape[1]
    out_ref[:, :dim] = query_ref[...]
    line = lax.broadcasted_iota(jnp.int32, (ROWS, TAIL), 0)
    lane = lax.broadcasted_iota(jnp.int32, (ROWS, TAIL), 1)
    index = jnp.zeros_like(line)
    for r in range(ROWS):
        index = jnp.where(line == r, pos_ref[r], index)
    coded = jnp.where(lane == 0, index // POS_BASE, jnp.where(lane == 1, index % POS_BASE, 0))
    out_ref[:, dim:] = coded.astype(f32).astype(bf16)


def split3(v):
    hi = v.astype(bf16)
    rest = v - hi.astype(f32)
    mid = rest.astype(bf16)
    return hi, mid, (rest - mid.astype(f32)).astype(bf16)


def exact_dot(v, onehot, dims):
    parts = [lax.dot_general(p, onehot, dims, preferred_element_type=f32) for p in split3(v)]
    return parts[0] + parts[1] + parts[2]


def batch_scores(first_slot, blocks, doc_ref, score_ref, query_ref, stat_ref, pos_ref, left_ref, tail_ref):
    half, dim = query_ref.shape
    at = 0
    for block in blocks:
        rows = block.shape[0]
        query_ref[at : at + rows, :] = block[:, :dim]
        tail_ref[at : at + rows, :] = block[:, dim:]
        at += rows
    lane = lax.broadcasted_iota(jnp.int32, (8, TAIL), 1)
    line = lax.broadcasted_iota(jnp.int32, (8, TAIL), 0)
    pick = jnp.where(lane == line, 1.0, 0.0).astype(bf16)
    parts = lax.dot_general(pick, tail_ref[...], contract_last, preferred_element_type=f32)
    positive = (parts[0:1] * POS_BASE + parts[1:2]).astype(jnp.int32) - first_slot
    pos_ref[...] = positive
    steps = doc_ref.shape[0] // TILE

    def multiply(t, top):
        at = pl.multiple_of(t * TILE, TILE)
        scores = sharpness_scale * lax.dot_general(
            doc_ref[pl.ds(at, TILE), :], query_ref[...], contract_last, preferred_element_type=f32
        )
        score_ref[pl.ds(at, TILE), :] = scores
        return jnp.maximum(top, jnp.max(scores, axis=0, keepdims=True))

    top = lax.fori_loop(0, steps, multiply, jnp.full((1, half), -jnp.inf, f32))
    wide = 2 * SUB
    lines = half // ROWS * wide
    line = lax.broadcasted_iota(jnp.int32, (lines, half), 0)
    lane = lax.broadcasted_iota(jnp.int32, (lines, half), 1)
    wanted = jnp.where(lane == line // wide * ROWS + line % SUB, 1.0, 0.0).astype(bf16)
    is_u = lax.broadcasted_iota(jnp.int32, (lines, TILE), 0) % wide < SUB

    def sums(t, carry):
        at = pl.multiple_of(t * TILE, TILE)
        scores = score_ref[pl.ds(at, TILE), :]
        hit = at + lax.broadcasted_iota(jnp.int32, scores.shape, 0) == positive
        exps = jnp.exp(scores - top)
        total = carry[0] + jnp.sum(exps, axis=0, keepdims=True)
        found = carry[1] + jnp.sum(jnp.where(hit, scores, 0.0), axis=0, keepdims=True)
        others = jnp.where(hit, 0.0, exps).astype(bf16)
        onehot = jnp.where(hit, 1.0, 0.0).astype(bf16)
        left_ref[:, pl.ds(at, TILE)] = jnp.where(
            is_u,
            lax.dot_general(wanted, others, contract_last, preferred_element_type=f32),
            lax.dot_general(wanted, onehot, contract_last, preferred_element_type=f32),
        ).astype(bf16)
        return total, found

    zero = jnp.zeros((1, half), f32)
    total, found = lax.fori_loop(0, steps, sums, (zero, zero))
    stat_ref[...] = jnp.concatenate([top, total, found, jnp.zeros((5, half), f32)], axis=0)


def first_kernel(blk_ref, *refs):
    blocks, refs = refs[:-10], refs[-10:]
    hidden_ref, gain_ref, doc_ref, normed_ref = refs[:4]
    hidden = hidden_ref[...].astype(f32)
    inv_rms = lax.rsqrt(jnp.mean(hidden * hidden, axis=1, keepdims=True) + epsilon)
    normed = hidden * inv_rms * gain_ref[...]
    normed_ref[...] = jnp.concatenate([normed, jnp.zeros((8 - SUB, hidden.shape[1]), f32)], axis=0).astype(bf16)
    batch_scores(blk_ref[0] * doc_ref.shape[0], blocks, doc_ref, *refs[4:])


def second_kernel(blk_ref, *refs):
    blocks, refs = refs[:-14], refs[-14:]
    stat_first, left_first, normed_ref, doc_ref, all_ref, sub_ref, order_ref = refs[:7]
    score_ref, query_ref, pos_ref, stat_ref, left_ref, tail_ref, acc = refs[7:]
    cols = order_ref.shape[0]
    lane = lax.broadcasted_iota(jnp.int32, (ROWS, cols), 1)
    line = lax.broadcasted_iota(jnp.int32, (ROWS, cols), 0)
    places = places_of(blk_ref[0])
    for k in range(N_BLK):
        order_ref[k * ROWS : (k + 1) * ROWS, :] = jnp.where(lane == places[k] * ROWS + line, 1.0, 0.0).astype(bf16)
    batch_scores(
        blk_ref[0] * doc_ref.shape[0], blocks, doc_ref, score_ref, query_ref, stat_ref, pos_ref, left_ref, tail_ref
    )
    stats = jnp.concatenate([stat_first[...], stat_ref[...]], axis=1)
    stats = exact_dot(stats, order_ref[...], (((1,), (0,)), ((), ())))
    parts = split3(stats)
    all_ref[...] = jnp.concatenate([p[:3].astype(f32) for p in parts] + [jnp.zeros((7, cols), f32)], axis=0).astype(bf16)
    four = 2 * SUB
    lines = N_BLK * WIDE
    line = lax.broadcasted_iota(jnp.int32, (lines, N_BLK * four), 0)
    lane = lax.broadcasted_iota(jnp.int32, (lines, N_BLK * four), 1)
    swap = jnp.zeros(line.shape, f32)
    for k in range(N_BLK):
        swap = jnp.where((lane // four == k) & (line == places[k] * WIDE + lane % four), 1.0, swap)
    left = jnp.concatenate([left_first[...], left_ref[...]], axis=0)
    left = jnp.dot(swap.astype(bf16), left, preferred_element_type=f32).astype(bf16)
    line = lax.broadcasted_iota(jnp.int32, (lines, 8), 0)
    lane = lax.broadcasted_iota(jnp.int32, (lines, 8), 1)
    spread = jnp.where((line % WIDE - four == lane) & (lane < SUB), 1.0, 0.0).astype(bf16)
    acc[...] = jnp.dot(spread, normed_ref[...], preferred_element_type=f32)
    acc[...] += jnp.dot(left, doc_ref[...], preferred_element_type=f32)
    line = lax.broadcasted_iota(jnp.int32, (lines, cols), 0)
    lane = lax.broadcasted_iota(jnp.int32, (lines, cols), 1)
    wanted = jnp.where((lane == line // WIDE * ROWS + line % WIDE) & (line % WIDE < SUB), 1.0, 0.0).astype(bf16)
    stat_rows = [
        lax.dot_general(wanted, p, contract_last, preferred_element_type=f32).astype(bf16) for p in parts
    ]
    width = doc_ref.shape[1] // N_GRP
    grads = acc[...].astype(bf16)
    tail = jnp.concatenate(stat_rows + [jnp.zeros((lines, LANES - width - 24), bf16)], axis=1)
    for g in range(N_GRP):
        sub_ref[g] = jnp.concatenate([grads[:, g * width : (g + 1) * width], tail], axis=1)


def cotangent_kernel(got_ref, stat_ref, cot_ref, width):
    rows = got_ref[:, :, : 2 * SUB, :].astype(f32)
    terms, hits, tail = rows[:, :, :SUB, :width], rows[:, :, SUB:, :width], rows[:, :, :SUB, width:]
    stat = lambda k: tail[..., k : k + 1] + tail[..., k + 8 : k + 9] + tail[..., k + 16 : k + 17]
    top = jnp.max(stat(0), axis=1, keepdims=True)
    total = jnp.sum(stat(1) * jnp.exp(stat(0) - top), axis=1, keepdims=True)
    log_total = top + jnp.log(total)
    found = jnp.sum(stat(2), axis=1, keepdims=True)
    scale = jnp.exp(stat(0) - log_total)
    grads = jnp.sum(scale * terms + (jnp.exp(found - log_total) - 1.0) * hits, axis=1)
    grads = sharpness_scale * grads
    grads = jnp.concatenate([grads[g] for g in range(N_GRP)], axis=0)
    grads = jnp.concatenate([grads, jnp.zeros((N_GRP * SUB, LANES - width), f32)], axis=1).astype(bf16)
    for b in range(N_BLK):
        cot_ref[b, : N_GRP * SUB] = grads
        cot_ref[b, N_GRP * SUB :] = stat_ref[...]


def weight_kernel(stats_ref, pos_a, pos_b, order_ref, first_ref, second_ref, query_a, query_b, loss_ref, grad_ref, total):
    step = pl.program_id(0)
    cols = order_ref.shape[1]
    half = cols // 2

    @pl.when(step == 0)
    def _():
        stats = stats_ref[:, N_GRP * SUB :, :].astype(f32)
        tops, totals, found = (stats[:, k] + stats[:, k + 3] + stats[:, k + 6] for k in range(3))
        top = jnp.max(tops, axis=0, keepdims=True)
        summed = jnp.sum(totals * jnp.exp(tops - top), axis=0, keepdims=True)
        log_total = top + jnp.log(summed)
        losses = log_total - jnp.sum(found, axis=0, keepdims=True)
        both = jnp.concatenate([log_total, losses, jnp.zeros((6, cols), f32)], axis=0)
        both = exact_dot(both, order_ref[...], contract_last)
        loss_ref[...] = both[1:2]
        total[...] = both[0:1]

    out = None
    for k, (score_ref, query_ref, pos_ref) in enumerate(
        ((first_ref, query_a, pos_a), (second_ref, query_b, pos_b))
    ):
        scores = score_ref[...]
        slot = step * scores.shape[0] + lax.broadcasted_iota(jnp.int32, scores.shape, 0)
        onehot = jnp.where(slot == pos_ref[...], 1.0, 0.0)
        weights = (jnp.exp(scores - total[:, k * half : (k + 1) * half]) - onehot).astype(bf16)
        term = jnp.dot(weights, query_ref[...], preferred_element_type=f32)
        out = term if out is None else out + term
    grad_ref[...] = (sharpness_scale * out).astype(bf16)


def passage_terms(stats, pos_a, pos_b, order, score_a, score_b, query_a, query_b):
    shard_rows, half = score_a.shape
    dim = query_a.shape[1]
    tile = 256
    fixed = lambda v: pl.BlockSpec(v.shape, lambda i: (0,) * v.ndim)
    return pl.pallas_call(
        weight_kernel,
        grid=(shard_rows // tile,),
        in_specs=[fixed(stats), fixed(pos_a), fixed(pos_b), fixed(order)]
        + [pl.BlockSpec((tile, half), lambda i: (i, 0))] * 2
        + [fixed(query_a), fixed(query_b)],
        out_specs=[
            pl.BlockSpec((1, 2 * half), lambda i: (0, 0)),
            pl.BlockSpec((tile, dim), lambda i: (i, 0)),
        ],
        out_shape=[
            jax.ShapeDtypeStruct((1, 2 * half), f32),
            jax.ShapeDtypeStruct((shard_rows, dim), bf16),
        ],
        scratch_shapes=[pltpu.VMEM((1, 2 * half), f32)],
        compiler_params=pltpu.CompilerParams(vmem_limit_bytes=32 * 1024 * 1024),
        cost_estimate=pl.CostEstimate(
            flops=4 * shard_rows * half * dim, bytes_accessed=4 * shard_rows * dim, transcendentals=0
        ),
        name="passage_terms",
    )(stats, pos_a, pos_b, order, score_a, score_b, query_a, query_b)


def act_kernel(blk_ref, cot_ref, got_ref, down_ref, gate_ref, up_ref, out_ref, normed):
    units, part = down_ref.shape
    for g in range(N_GRP):
        for b in range(N_BLK):
            at = (g * N_BLK + b) * SUB
            normed[at : at + SUB, :] = got_ref[g, b, 2 * SUB :, :part].astype(f32)
    rows = cot_ref[:, : N_GRP * SUB, :].reshape(-1, LANES)
    count = rows.shape[0]
    line = lax.broadcasted_iota(jnp.int32, (count, count), 0)
    lane = lax.broadcasted_iota(jnp.int32, (count, count), 1)
    per = N_BLK * SUB
    swap = jnp.where(lane == (line % per // SUB * N_GRP + line // per) * SUB + line % SUB, 1.0, 0.0).astype(bf16)
    rows = jnp.dot(swap, rows, preferred_element_type=f32).astype(bf16)[:, :part]
    values = [lax.dot_general(rows, down_ref[...], contract_last, preferred_element_type=f32).astype(bf16)]
    rows = normed[...].astype(bf16)
    values.append(jnp.dot(rows, gate_ref[...], preferred_element_type=f32).astype(bf16))
    values.append(jnp.dot(rows, up_ref[...], preferred_element_type=f32).astype(bf16))
    own = cot_ref[blk_ref[0]]
    width = part // N_GRP
    blank = jnp.zeros((per - N_GRP * SUB, width), bf16)
    for g in range(N_GRP):
        mine = own[g * SUB : (g + 1) * SUB].astype(f32)
        pieces = [mine[:, k * width : (k + 1) * width] for k in range(N_GRP)]
        pieces = jnp.concatenate(pieces, axis=0).astype(bf16)
        for k in range(3):
            out_ref[g, k * per : (k + 1) * per, :units] = values[k][g * per : (g + 1) * per]
        out_ref[g, :per, units : units + width] = jnp.concatenate([pieces, blank], axis=0)
        out_ref[g, per:, units : units + width] = jnp.zeros((2 * per, width), bf16)


def swiglu_kernel(got_ref, out_ref, cot_ref):
    per = got_ref.shape[1] // 3
    units = out_ref.shape[2]
    sums = jnp.sum(got_ref[:, :, :units].astype(f32), axis=0)
    act_grad, gate_value, up_value = sums[:per], sums[per : 2 * per], sums[2 * per :]
    gate_sigmoid = jax.nn.sigmoid(gate_value)
    up_grad = (act_grad * gate_value * gate_sigmoid).astype(bf16)
    gate_grad = (act_grad * up_value * gate_sigmoid * (1.0 + gate_value * (1.0 - gate_sigmoid))).astype(bf16)
    for g in range(N_GRP):
        out_ref[g, :per] = gate_grad
        out_ref[g, per:] = up_grad
    pieces = got_ref[:, : N_GRP * SUB, units:].astype(f32)
    cot_ref[...] = jnp.concatenate(
        [pieces[g, k * SUB : (k + 1) * SUB] for g in range(N_GRP) for k in range(N_GRP)], axis=1
    )


def backward_kernel(grad_ref, gate_ref, up_ref, out_ref):
    per = grad_ref.shape[1] // 2
    both = grad_ref[...]
    gate_grad = both[:, :per].reshape(N_GRP * per, -1)
    up_grad = both[:, per:].reshape(N_GRP * per, -1)
    total = lax.dot_general(gate_grad, gate_ref[...], contract_last, preferred_element_type=f32)
    total += lax.dot_general(up_grad, up_ref[...], contract_last, preferred_element_type=f32)
    for g in range(N_GRP):
        out_ref[g] = total[g * per : (g + 1) * per].astype(bf16)


def hidden_kernel(back_ref, cot_ref, hidden_ref, gain_ref, out_ref):
    sums = jnp.sum(back_ref[...].astype(f32), axis=1)
    normed_grad = jnp.concatenate([sums[g] for g in range(N_GRP)], axis=1)
    hidden = hidden_ref[...].astype(f32)
    inv_rms = lax.rsqrt(jnp.mean(hidden * hidden, axis=1, keepdims=True) + epsilon)
    scaled = normed_grad * gain_ref[...]
    mean = jnp.mean(hidden * scaled, axis=1, keepdims=True)
    out_ref[...] = cot_ref[...] + inv_rms * scaled - hidden * inv_rms * inv_rms * inv_rms * mean


def exchange(v, axis):
    return lax.all_to_all(v, axis, 0, 0, tiled=True)


def shards(
    queries, stored_documents, positive, last_hidden, norm_gain, gate_weight, up_weight, down_weight
):
    shape = jax.ShapeDtypeStruct
    blk = lax.axis_index("blk").astype(jnp.int32)[None]
    shard_rows, dim = stored_documents.shape
    part = dim // N_GRP
    units = gate_weight.shape[1]
    cols = N_BLK * ROWS
    half = cols // 2
    per = N_BLK * SUB
    gain = norm_gain[None]

    block = local(block_kernel, "block", shape((ROWS, dim + TAIL), bf16), scalars=1, count=1)(
        positive, queries
    )
    first = near_column(block)
    second = far_column(*first[1:4])

    product = 2 * shard_rows * half * dim
    normed, score_a, query_a, stat_a, pos_a, left_a = local(
        first_kernel,
        "first_scores",
        [
            shape((8, dim), bf16),
            shape((shard_rows, half), f32),
            shape((half, dim), bf16),
            shape((8, half), f32),
            shape((1, half), jnp.int32),
            shape((per, shard_rows), bf16),
        ],
        scratch=[pltpu.VMEM((half, TAIL), bf16)],
        scalars=1,
        count=len(first) + 3,
        flops=2 * product,
        moved=4 * shard_rows * dim,
    )(blk, *first, last_hidden, gain, stored_documents)
    second, left_a = lax.optimization_barrier((second, left_a))
    second = far_rest(*second, ROWS // 2)
    stats, sub_terms, order, score_b, query_b, pos_b = local(
        second_kernel,
        "second_scores",
        [
            shape((16, cols), bf16),
            shape((N_GRP, N_BLK * WIDE, LANES), bf16),
            shape((cols, cols), bf16),
            shape((shard_rows, half), f32),
            shape((half, dim), bf16),
            shape((1, half), jnp.int32),
        ],
        scratch=[
            pltpu.VMEM((8, half), f32),
            pltpu.VMEM((per, shard_rows), bf16),
            pltpu.VMEM((half, TAIL), bf16),
            pltpu.VMEM((N_BLK * WIDE, dim), f32),
        ],
        scalars=1,
        count=len(second) + 4,
        flops=2 * product,
        moved=4 * shard_rows * dim,
    )(blk, *second, stat_a, left_a, normed, stored_documents)

    got = exchange(sub_terms.reshape(N_GRP * N_BLK, WIDE, LANES), ("grp", "blk"))
    got = got.reshape(N_GRP, N_BLK, WIDE, LANES)
    cot = local(
        functools.partial(cotangent_kernel, width=part),
        "cotangents",
        shape((N_BLK, 2 * N_GRP * SUB, LANES), bf16),
        count=2,
    )(got, stats)
    cot = exchange(cot, "blk")

    loss_row, passage_part = passage_terms(cot, pos_a, pos_b, order, score_a, score_b, query_a, query_b)
    losses = loss_row[0, :ROWS]
    cot, passage_part = lax.optimization_barrier((cot, passage_part))
    passage_sum = lax.psum_scatter(passage_part, "grp", scatter_dimension=0, tiled=True)

    values = local(
        act_kernel,
        "act",
        shape((N_GRP, 3 * per, units + part // N_GRP), bf16),
        scratch=[pltpu.VMEM((N_GRP * per, part), f32)],
        scalars=1,
        count=5,
    )(blk, cot, got, down_weight, gate_weight, up_weight)
    grads, cotangent = local(
        swiglu_kernel,
        "swiglu",
        [shape((N_GRP, 2 * per, units), bf16), shape((SUB, dim), f32)],
        count=1,
    )(exchange(values, "grp"))
    normed_part = local(backward_kernel, "backward", shape((N_GRP, per, part), bf16), count=3)(
        exchange(grads, "grp"), gate_weight, up_weight
    )
    back = exchange(normed_part.reshape(N_GRP * N_BLK, SUB, part), ("grp", "blk"))
    passage_grads = passage_sum.astype(f32)
    hidden_grads = local(hidden_kernel, "hidden", shape((SUB, dim), f32), count=4)(
        back.reshape(N_GRP, N_BLK, SUB, part), cotangent, last_hidden, gain
    )
    return (losses, passage_grads, hidden_grads)


def solution(mesh):
    return jax.shard_map(
        shards,
        mesh=mesh,
        in_specs=(
            P(("blk", "grp"), None),
            P("blk", None),
            P(("blk", "grp")),
            P(("blk", "grp"), None),
            P(),
            P("grp", "blk"),
            P("grp", "blk"),
            P("blk", "grp"),
        ),
        out_specs=(P(("blk", "grp")), P(("blk", "grp"), None), P(("blk", "grp"), None)),
        check_vma=False,
    )
```

```python
import functools

import jax
import jax.numpy as jnp
from jax import lax
from jax.experimental import pallas as pl
from jax.experimental.pallas import tpu as pltpu
from jax.sharding import PartitionSpec as P

sharpness_scale = 20.0
epsilon = 1e-06
contract_last = (((1,), (1,)), ((), ()))
Z, X, C = 4, 2, 2
N_BLK, N_GRP = 16, 8
POS_BASE = 128
TAIL = 128
ROWS = 32
SUB = 2
WIDE = 3 * SUB
LANES = 512
Y_FIRST = 2816
GX, GY = 2, 4
Y_GROUPS = [[x * GY + y for y in range(GY)] for x in range(GX)]
TILE = 256
f32, bf16 = jnp.float32, jnp.bfloat16
VMEM = pl.BlockSpec(memory_space=pltpu.VMEM)
SMEM = pl.BlockSpec(memory_space=pltpu.SMEM)


def local(kernel, name, out_shape, scratch=(), scalars=0, count=0, flops=0, moved=0, vmem=32):
    return pl.pallas_call(
        kernel,
        in_specs=[SMEM] * scalars + [VMEM] * count,
        out_specs=jax.tree.map(lambda _: VMEM, out_shape),
        out_shape=out_shape,
        scratch_shapes=list(scratch),
        compiler_params=pltpu.CompilerParams(vmem_limit_bytes=vmem * 1024 * 1024),
        cost_estimate=pl.CostEstimate(flops=flops, bytes_accessed=moved, transcendentals=0),
        name=name,
    )


def blk_shift(dz, dx, dc):
    pairs = []
    for s in range(N_BLK):
        z, x, c = s // (X * C), s // C % X, s % C
        pairs.append((s, ((z + dz) % Z * X + (x + dx) % X) * C + (c + dc) % C))
    return pairs


def send(v, *shift):
    return lax.ppermute(v, "blk", blk_shift(*shift))


def near_column(block):
    own = [block, send(block, 1, 0, 0), send(block, -1, 0, 0), send(block, 0, 1, 0)]
    return own + [send(v, 0, 0, 1) for v in own]


def far_column(below, above, across):
    across_below = send(across, 1, 0, 0)
    far = send(above, -1, 0, 0)
    across_above = send(above, 0, 1, 0)
    return across_below, far, across_above


def far_rest(across_below, far, across_above, half):
    own = [
        across_below,
        far,
        across_above,
        send(across_below[:half], 1, 0, 0),
        send(far[half:], 0, 1, 0),
    ]
    return own + [send(v, 0, 0, 1) for v in own]


def places_of(blk):
    z, x, c = blk // (X * C), blk // C % X, blk % C
    shifts = [(0, 0), (-1, 0), (1, 0), (0, 1)], [(-1, 1), (2, 0), (1, 1), (2, 1)]
    return [
        ((z + dz + Z) % Z * X + (x + dx) % X) * C + (c + dc) % C
        for batch in shifts
        for dc in range(C)
        for dz, dx in batch
    ]


def block_kernel(pos_ref, query_ref, out_ref):
    dim = query_ref.shape[1]
    out_ref[:, :dim] = query_ref[...]
    line = lax.broadcasted_iota(jnp.int32, (ROWS, TAIL), 0)
    lane = lax.broadcasted_iota(jnp.int32, (ROWS, TAIL), 1)
    index = jnp.zeros_like(line)
    for r in range(ROWS):
        index = jnp.where(line == r, pos_ref[r], index)
    coded = jnp.where(lane == 0, index // POS_BASE, jnp.where(lane == 1, index % POS_BASE, 0))
    out_ref[:, dim:] = coded.astype(f32).astype(bf16)


def split3(v):
    hi = v.astype(bf16)
    rest = v - hi.astype(f32)
    mid = rest.astype(bf16)
    return hi, mid, (rest - mid.astype(f32)).astype(bf16)


def exact_dot(v, onehot, dims):
    parts = [lax.dot_general(p, onehot, dims, preferred_element_type=f32) for p in split3(v)]
    return parts[0] + parts[1] + parts[2]


def batch_scores(first_slot, blocks, doc_ref, score_ref, query_ref, stat_ref, pos_ref, left_ref, tail_ref):
    half, dim = query_ref.shape
    at = 0
    for block in blocks:
        rows = block.shape[0]
        query_ref[at : at + rows, :] = block[:, :dim]
        tail_ref[at : at + rows, :] = block[:, dim:]
        at += rows
    lane = lax.broadcasted_iota(jnp.int32, (8, TAIL), 1)
    line = lax.broadcasted_iota(jnp.int32, (8, TAIL), 0)
    pick = jnp.where(lane == line, 1.0, 0.0).astype(bf16)
    parts = lax.dot_general(pick, tail_ref[...], contract_last, preferred_element_type=f32)
    positive = (parts[0:1] * POS_BASE + parts[1:2]).astype(jnp.int32) - first_slot
    pos_ref[...] = positive
    steps = doc_ref.shape[0] // TILE

    def multiply(t, top):
        at = pl.multiple_of(t * TILE, TILE)
        scores = sharpness_scale * lax.dot_general(
            doc_ref[pl.ds(at, TILE), :], query_ref[...], contract_last, preferred_element_type=f32
        )
        score_ref[pl.ds(at, TILE), :] = scores
        return jnp.maximum(top, jnp.max(scores, axis=0, keepdims=True))

    top = lax.fori_loop(0, steps, multiply, jnp.full((1, half), -jnp.inf, f32))
    wide = 2 * SUB
    lines = half // ROWS * wide
    line = lax.broadcasted_iota(jnp.int32, (lines, half), 0)
    lane = lax.broadcasted_iota(jnp.int32, (lines, half), 1)
    wanted = jnp.where(lane == line // wide * ROWS + line % SUB, 1.0, 0.0).astype(bf16)
    is_u = lax.broadcasted_iota(jnp.int32, (lines, TILE), 0) % wide < SUB

    def sums(t, carry):
        at = pl.multiple_of(t * TILE, TILE)
        scores = score_ref[pl.ds(at, TILE), :]
        hit = at + lax.broadcasted_iota(jnp.int32, scores.shape, 0) == positive
        exps = jnp.exp(scores - top)
        total = carry[0] + jnp.sum(exps, axis=0, keepdims=True)
        found = carry[1] + jnp.sum(jnp.where(hit, scores, 0.0), axis=0, keepdims=True)
        others = jnp.where(hit, 0.0, exps).astype(bf16)
        onehot = jnp.where(hit, 1.0, 0.0).astype(bf16)
        left_ref[:, pl.ds(at, TILE)] = jnp.where(
            is_u,
            lax.dot_general(wanted, others, contract_last, preferred_element_type=f32),
            lax.dot_general(wanted, onehot, contract_last, preferred_element_type=f32),
        ).astype(bf16)
        return total, found

    zero = jnp.zeros((1, half), f32)
    total, found = lax.fori_loop(0, steps, sums, (zero, zero))
    stat_ref[...] = jnp.concatenate([top, total, found, jnp.zeros((5, half), f32)], axis=0)


def first_kernel(blk_ref, *refs):
    blocks, refs = refs[:-10], refs[-10:]
    hidden_ref, gain_ref, doc_ref, normed_ref = refs[:4]
    hidden = hidden_ref[...].astype(f32)
    inv_rms = lax.rsqrt(jnp.mean(hidden * hidden, axis=1, keepdims=True) + epsilon)
    normed = hidden * inv_rms * gain_ref[...]
    normed_ref[...] = jnp.concatenate([normed, jnp.zeros((8 - SUB, hidden.shape[1]), f32)], axis=0).astype(bf16)
    batch_scores(blk_ref[0] * doc_ref.shape[0], blocks, doc_ref, *refs[4:])


def second_kernel(blk_ref, *refs):
    blocks, refs = refs[:-14], refs[-14:]
    stat_first, left_first, normed_ref, doc_ref, all_ref, sub_ref, order_ref = refs[:7]
    score_ref, query_ref, pos_ref, stat_ref, left_ref, tail_ref, acc = refs[7:]
    cols = order_ref.shape[0]
    lane = lax.broadcasted_iota(jnp.int32, (ROWS, cols), 1)
    line = lax.broadcasted_iota(jnp.int32, (ROWS, cols), 0)
    places = places_of(blk_ref[0])
    for k in range(N_BLK):
        order_ref[k * ROWS : (k + 1) * ROWS, :] = jnp.where(lane == places[k] * ROWS + line, 1.0, 0.0).astype(bf16)
    batch_scores(
        blk_ref[0] * doc_ref.shape[0], blocks, doc_ref, score_ref, query_ref, stat_ref, pos_ref, left_ref, tail_ref
    )
    stats = jnp.concatenate([stat_first[...], stat_ref[...]], axis=1)
    stats = exact_dot(stats, order_ref[...], (((1,), (0,)), ((), ())))
    all_ref[...] = stats
    parts = split3(stats)
    four = 2 * SUB
    lines = N_BLK * WIDE
    line = lax.broadcasted_iota(jnp.int32, (lines, N_BLK * four), 0)
    lane = lax.broadcasted_iota(jnp.int32, (lines, N_BLK * four), 1)
    swap = jnp.zeros(line.shape, f32)
    for k in range(N_BLK):
        swap = jnp.where((lane // four == k) & (line == places[k] * WIDE + lane % four), 1.0, swap)
    left = jnp.concatenate([left_first[...], left_ref[...]], axis=0)
    left = jnp.dot(swap.astype(bf16), left, preferred_element_type=f32).astype(bf16)
    line = lax.broadcasted_iota(jnp.int32, (lines, 8), 0)
    lane = lax.broadcasted_iota(jnp.int32, (lines, 8), 1)
    spread = jnp.where((line % WIDE - four == lane) & (lane < SUB), 1.0, 0.0).astype(bf16)
    acc[...] = jnp.dot(spread, normed_ref[...], preferred_element_type=f32)
    acc[...] += jnp.dot(left, doc_ref[...], preferred_element_type=f32)
    line = lax.broadcasted_iota(jnp.int32, (lines, cols), 0)
    lane = lax.broadcasted_iota(jnp.int32, (lines, cols), 1)
    wanted = jnp.where((lane == line // WIDE * ROWS + line % WIDE) & (line % WIDE < SUB), 1.0, 0.0).astype(bf16)
    stat_rows = [
        lax.dot_general(wanted, p, contract_last, preferred_element_type=f32).astype(bf16) for p in parts
    ]
    width = doc_ref.shape[1] // N_GRP
    grads = acc[...].astype(bf16)
    tail = jnp.concatenate(stat_rows + [jnp.zeros((lines, LANES - width - 24), bf16)], axis=1)
    for g in range(N_GRP):
        sub_ref[g] = jnp.concatenate([grads[:, g * width : (g + 1) * width], tail], axis=1)


def merge_kernel(*refs):
    refs, out_ref = refs[:-1], refs[-1]
    top = functools.reduce(jnp.maximum, [r[0:1] for r in refs])
    total = sum(r[1:2] * jnp.exp(r[0:1] - top) for r in refs)
    found = sum(r[2:3] for r in refs)
    out_ref[...] = jnp.concatenate([top, total, found, jnp.zeros_like(out_ref[3:])], axis=0)


def cotangent_kernel(got_ref, cot_ref):
    width = cot_ref.shape[2]
    rows = got_ref[:, :, : 2 * SUB, :].astype(f32)
    terms, hits, tail = rows[:, :, :SUB, :width], rows[:, :, SUB:, :width], rows[:, :, :SUB, width:]
    stat = lambda k: tail[..., k : k + 1] + tail[..., k + 8 : k + 9] + tail[..., k + 16 : k + 17]
    top = jnp.max(stat(0), axis=1, keepdims=True)
    total = jnp.sum(stat(1) * jnp.exp(stat(0) - top), axis=1, keepdims=True)
    log_total = top + jnp.log(total)
    found = jnp.sum(stat(2), axis=1, keepdims=True)
    scale = jnp.exp(stat(0) - log_total)
    grads = jnp.sum(scale * terms + (jnp.exp(found - log_total) - 1.0) * hits, axis=1)
    grads = sharpness_scale * grads
    grads = jnp.concatenate([grads[g] for g in range(N_GRP)], axis=0).astype(bf16)
    for b in range(N_BLK):
        cot_ref[b] = grads


def weight_kernel(grp_ref, stats_ref, pos_a, pos_b, order_ref, first_ref, second_ref, query_a, query_b, *refs):
    loss_ref, whole_ref, own_ref, other_ref, total = refs
    step = pl.program_id(0)
    cols = order_ref.shape[1]
    half = cols // 2

    @pl.when(step == 0)
    def _():
        log_total = stats_ref[0:1] + jnp.log(stats_ref[1:2])
        losses = log_total - stats_ref[2:3]
        both = jnp.concatenate([log_total, losses, jnp.zeros((6, cols), f32)], axis=0)
        both = exact_dot(both, order_ref[...], contract_last)
        loss_ref[...] = both[1:2]
        total[...] = both[0:1]

    rows = first_ref.shape[2]
    out = None
    for k, (score_ref, query_ref, pos_ref) in enumerate(
        ((first_ref, query_a, pos_a), (second_ref, query_b, pos_b))
    ):
        scores = score_ref[...].reshape(GX * rows, half)
        line = lax.broadcasted_iota(jnp.int32, scores.shape, 0)
        slot = (line // rows * GY + step) * rows + line % rows
        onehot = jnp.where(slot == pos_ref[...], 1.0, 0.0)
        weights = (jnp.exp(scores - total[:, k * half : (k + 1) * half]) - onehot).astype(bf16)
        term = jnp.dot(weights, query_ref[...], preferred_element_type=f32)
        out = term if out is None else out + term
    out = sharpness_scale * out
    first_x = grp_ref[0] // GY == 0
    whole_ref[...] = out[:, :Y_FIRST].astype(bf16)
    own_ref[...] = jnp.where(first_x, out[:rows, Y_FIRST:], out[rows:, Y_FIRST:]).astype(bf16)
    other_ref[...] = jnp.where(first_x, out[rows:, Y_FIRST:], out[:rows, Y_FIRST:]).astype(bf16)


def passage_terms(grp, stats, pos_a, pos_b, order, score_a, score_b, query_a, query_b):
    shard_rows, half = score_a.shape
    dim = query_a.shape[1]
    rows = shard_rows // N_GRP
    shape = jax.ShapeDtypeStruct
    fixed = lambda v: pl.BlockSpec(v.shape, lambda i: (0,) * len(v.shape))
    scores = pl.BlockSpec((GX, 1, rows, half), lambda i: (0, i, 0, 0))
    apart = pl.BlockSpec((rows, dim - Y_FIRST), lambda i: (i, 0))
    loss = shape((1, 2 * half), f32)
    return pl.pallas_call(
        weight_kernel,
        grid=(GY,),
        in_specs=[SMEM, fixed(stats), fixed(pos_a), fixed(pos_b), fixed(order), scores, scores]
        + [fixed(query_a), fixed(query_b)],
        out_specs=[fixed(loss), pl.BlockSpec((GX * rows, Y_FIRST), lambda i: (i, 0)), apart, apart],
        out_shape=[loss, shape((shard_rows, Y_FIRST), bf16)]
        + [shape((GY * rows, dim - Y_FIRST), bf16)] * 2,
        scratch_shapes=[pltpu.VMEM((1, 2 * half), f32)],
        compiler_params=pltpu.CompilerParams(vmem_limit_bytes=52 * 1024 * 1024),
        cost_estimate=pl.CostEstimate(
            flops=4 * shard_rows * half * dim, bytes_accessed=4 * shard_rows * dim, transcendentals=0
        ),
        name="passage_terms",
    )(
        grp,
        stats,
        pos_a,
        pos_b,
        order,
        score_a.reshape(GX, GY, rows, half),
        score_b.reshape(GX, GY, rows, half),
        query_a,
        query_b,
    )


def x_sum_kernel(own_ref, got_ref, out_ref):
    out_ref[...] = (own_ref[...].astype(f32) + got_ref[...].astype(f32)).astype(bf16)


def x_split_kernel(grp_ref, both_ref, own_ref, other_ref):
    rows = own_ref.shape[0]
    first_x = grp_ref[0] // GY == 0
    above, below = both_ref[:rows].astype(f32), both_ref[rows:].astype(f32)
    own_ref[...] = jnp.where(first_x, above, below).astype(bf16)
    other_ref[...] = jnp.where(first_x, below, above).astype(bf16)


def passage_kernel(own_ref, got_ref, rest_ref, out_ref):
    out_ref[:, :Y_FIRST] = own_ref[...].astype(f32) + got_ref[...].astype(f32)
    out_ref[:, Y_FIRST:] = rest_ref[...].astype(f32)


def send_x(v):
    return lax.ppermute(v, "grp", [(g, (g + GY) % N_GRP) for g in range(N_GRP)])


def y_sum(v):
    return lax.psum_scatter(v, "grp", scatter_dimension=0, axis_index_groups=Y_GROUPS, tiled=True)


def act_kernel(blk_ref, cot_ref, got_ref, down_ref, gate_ref, up_ref, out_ref, normed):
    part, units = down_ref.shape
    for g in range(N_GRP):
        for b in range(N_BLK):
            at = (g * N_BLK + b) * SUB
            normed[at : at + SUB, :] = got_ref[g, b, 2 * SUB :, :part].astype(f32)
    rows = cot_ref[...].reshape(-1, part)
    count = rows.shape[0]
    line = lax.broadcasted_iota(jnp.int32, (count, count), 0)
    lane = lax.broadcasted_iota(jnp.int32, (count, count), 1)
    per = N_BLK * SUB
    swap = jnp.where(lane == (line % per // SUB * N_GRP + line // per) * SUB + line % SUB, 1.0, 0.0).astype(bf16)
    rows = jnp.dot(swap, rows, preferred_element_type=f32).astype(bf16)
    values = [jnp.dot(rows, down_ref[...], preferred_element_type=f32).astype(bf16)]
    rows = normed[...].astype(bf16)
    values.append(jnp.dot(rows, gate_ref[...], preferred_element_type=f32).astype(bf16))
    values.append(jnp.dot(rows, up_ref[...], preferred_element_type=f32).astype(bf16))
    own = cot_ref[blk_ref[0]]
    width = part // N_GRP
    blank = jnp.zeros((per - N_GRP * SUB, width), bf16)
    for g in range(N_GRP):
        mine = own[g * SUB : (g + 1) * SUB].astype(f32)
        pieces = [mine[:, k * width : (k + 1) * width] for k in range(N_GRP)]
        pieces = jnp.concatenate(pieces, axis=0).astype(bf16)
        for k in range(3):
            out_ref[g, k * per : (k + 1) * per, :units] = values[k][g * per : (g + 1) * per]
        out_ref[g, :per, units : units + width] = jnp.concatenate([pieces, blank], axis=0)
        out_ref[g, per:, units : units + width] = jnp.zeros((2 * per, width), bf16)


def swiglu_kernel(got_ref, out_ref, cot_ref):
    per = got_ref.shape[1] // 3
    units = out_ref.shape[2]
    sums = jnp.sum(got_ref[:, :, :units].astype(f32), axis=0)
    act_grad, gate_value, up_value = sums[:per], sums[per : 2 * per], sums[2 * per :]
    gate_sigmoid = jax.nn.sigmoid(gate_value)
    up_grad = (act_grad * gate_value * gate_sigmoid).astype(bf16)
    gate_grad = (act_grad * up_value * gate_sigmoid * (1.0 + gate_value * (1.0 - gate_sigmoid))).astype(bf16)
    for g in range(N_GRP):
        out_ref[g, :per] = gate_grad
        out_ref[g, per:] = up_grad
    pieces = got_ref[:, : N_GRP * SUB, units:].astype(f32)
    cot_ref[...] = jnp.concatenate(
        [pieces[g, k * SUB : (k + 1) * SUB] for g in range(N_GRP) for k in range(N_GRP)], axis=1
    )


def backward_kernel(grad_ref, gate_ref, up_ref, out_ref):
    per = grad_ref.shape[1] // 2
    both = grad_ref[...]
    gate_grad = both[:, :per].reshape(N_GRP * per, -1)
    up_grad = both[:, per:].reshape(N_GRP * per, -1)
    total = lax.dot_general(gate_grad, gate_ref[...], contract_last, preferred_element_type=f32)
    total += lax.dot_general(up_grad, up_ref[...], contract_last, preferred_element_type=f32)
    for g in range(N_GRP):
        out_ref[g] = total[g * per : (g + 1) * per].astype(bf16)


def hidden_kernel(back_ref, cot_ref, hidden_ref, gain_ref, out_ref):
    sums = jnp.sum(back_ref[...].astype(f32), axis=1)
    normed_grad = jnp.concatenate([sums[g] for g in range(N_GRP)], axis=1)
    hidden = hidden_ref[...].astype(f32)
    inv_rms = lax.rsqrt(jnp.mean(hidden * hidden, axis=1, keepdims=True) + epsilon)
    scaled = normed_grad * gain_ref[...]
    mean = jnp.mean(hidden * scaled, axis=1, keepdims=True)
    out_ref[...] = cot_ref[...] + inv_rms * scaled - hidden * inv_rms * inv_rms * inv_rms * mean


def exchange(v, axis):
    return lax.all_to_all(v, axis, 0, 0, tiled=True)


def shards(
    queries, stored_documents, positive, last_hidden, norm_gain, gate_weight, up_weight, down_weight
):
    shape = jax.ShapeDtypeStruct
    blk = lax.axis_index("blk").astype(jnp.int32)[None]
    grp = lax.axis_index("grp").astype(jnp.int32)[None]
    shard_rows, dim = stored_documents.shape
    part = dim // N_GRP
    units = gate_weight.shape[1]
    cols = N_BLK * ROWS
    half = cols // 2
    per = N_BLK * SUB
    gain = norm_gain[None]

    block = local(block_kernel, "block", shape((ROWS, dim + TAIL), bf16), scalars=1, count=1)(
        positive, queries
    )
    first = near_column(block)
    second = far_column(*first[1:4])

    product = 2 * shard_rows * half * dim
    normed, score_a, query_a, stat_a, pos_a, left_a = local(
        first_kernel,
        "first_scores",
        [
            shape((8, dim), bf16),
            shape((shard_rows, half), f32),
            shape((half, dim), bf16),
            shape((8, half), f32),
            shape((1, half), jnp.int32),
            shape((per, shard_rows), bf16),
        ],
        scratch=[pltpu.VMEM((half, TAIL), bf16)],
        scalars=1,
        count=len(first) + 3,
        flops=2 * product,
        moved=4 * shard_rows * dim,
    )(blk, *first, last_hidden, gain, stored_documents)
    second, left_a = lax.optimization_barrier((second, left_a))
    second = far_rest(*second, ROWS // 2)
    stats, sub_terms, order, score_b, query_b, pos_b = local(
        second_kernel,
        "second_scores",
        [
            shape((8, cols), f32),
            shape((N_GRP, N_BLK * WIDE, LANES), bf16),
            shape((cols, cols), bf16),
            shape((shard_rows, half), f32),
            shape((half, dim), bf16),
            shape((1, half), jnp.int32),
        ],
        scratch=[
            pltpu.VMEM((8, half), f32),
            pltpu.VMEM((per, shard_rows), bf16),
            pltpu.VMEM((half, TAIL), bf16),
            pltpu.VMEM((N_BLK * WIDE, dim), f32),
        ],
        scalars=1,
        count=len(second) + 4,
        flops=2 * product,
        moved=4 * shard_rows * dim,
    )(blk, *second, stat_a, left_a, normed, stored_documents)

    got = exchange(sub_terms.reshape(N_GRP * N_BLK, WIDE, LANES), ("grp", "blk"))
    for steps in ([(0, 1, 0), (0, 0, 1), (0, 1, 1)], [(1, 0, 0), (2, 0, 0), (3, 0, 0)]):
        stats = local(merge_kernel, "merge", shape((8, cols), f32), count=4)(
            stats, *[send(stats, *step) for step in steps]
        )
    loss_row, whole, own, other = passage_terms(
        grp, stats, pos_a, pos_b, order, score_a, score_b, query_a, query_b
    )
    losses = loss_row[0, :ROWS]
    got = got.reshape(N_GRP, N_BLK, WIDE, LANES)
    cot = local(cotangent_kernel, "cotangents", shape((N_BLK, N_GRP * SUB, part), bf16), count=1)(got)
    cot, whole, other = lax.optimization_barrier((cot, whole, other))
    other = send_x(other)
    whole = y_sum(whole)
    cot = exchange(cot, "blk")

    values = local(
        act_kernel,
        "act",
        shape((N_GRP, 3 * per, units + part // N_GRP), bf16),
        scratch=[pltpu.VMEM((N_GRP * per, part), f32)],
        scalars=1,
        count=5,
    )(blk, cot, got, down_weight.T, gate_weight, up_weight)
    grads, cotangent = local(
        swiglu_kernel,
        "swiglu",
        [shape((N_GRP, 2 * per, units), bf16), shape((SUB, dim), f32)],
        count=1,
    )(exchange(values, "grp"))
    grads, other = lax.optimization_barrier((grads, other))
    rest = local(x_sum_kernel, "x_sum", shape(own.shape, bf16), count=2)(own, other)
    grads, rest = lax.optimization_barrier((grads, rest))
    rest = y_sum(rest)
    normed_part = local(backward_kernel, "backward", shape((N_GRP, per, part), bf16), count=3)(
        exchange(grads, "grp"), gate_weight, up_weight
    )
    normed_part, whole = lax.optimization_barrier((normed_part, whole))
    own, other = local(
        x_split_kernel, "x_split", [shape((shard_rows // N_GRP, Y_FIRST), bf16)] * 2, scalars=1, count=1
    )(grp, whole)
    normed_part, other = lax.optimization_barrier((normed_part, other))
    other = send_x(other)
    back = exchange(normed_part.reshape(N_GRP * N_BLK, SUB, part), ("grp", "blk"))
    passage_grads = local(passage_kernel, "passages", shape((shard_rows // N_GRP, dim), f32), count=3)(
        own, other, rest
    )
    hidden_grads = local(hidden_kernel, "hidden", shape((SUB, dim), f32), count=4)(
        back.reshape(N_GRP, N_BLK, SUB, part), cotangent, last_hidden, gain
    )
    return (losses, passage_grads, hidden_grads)


def solution(mesh):
    return jax.shard_map(
        shards,
        mesh=mesh,
        in_specs=(
            P(("blk", "grp"), None),
            P("blk", None),
            P(("blk", "grp")),
            P(("blk", "grp"), None),
            P(),
            P("grp", "blk"),
            P("grp", "blk"),
            P("blk", "grp"),
        ),
        out_specs=(P(("blk", "grp")), P(("blk", "grp"), None), P(("blk", "grp"), None)),
        check_vma=False,
    )
```

```python
import functools

import jax
import jax.numpy as jnp
from jax import lax
from jax.experimental import pallas as pl
from jax.experimental.pallas import tpu as pltpu
from jax.sharding import PartitionSpec as P

sharpness_scale = 20.0
epsilon = 1e-06
contract_last = (((1,), (1,)), ((), ()))
Z, X, C = 4, 2, 2
N_BLK, N_GRP = 16, 8
POS_BASE = 128
TAIL = 128
ROWS = 32
SUB = 2
WIDE = 3 * SUB
LANES = 512
Y_FIRST = 2688
GX, GY = 2, 4
Y_GROUPS = [[x * GY + y for y in range(GY)] for x in range(GX)]
TILE = 256
f32, bf16 = jnp.float32, jnp.bfloat16
VMEM = pl.BlockSpec(memory_space=pltpu.VMEM)
SMEM = pl.BlockSpec(memory_space=pltpu.SMEM)


def local(kernel, name, out_shape, scratch=(), scalars=0, count=0, flops=0, moved=0, vmem=32):
    return pl.pallas_call(
        kernel,
        in_specs=[SMEM] * scalars + [VMEM] * count,
        out_specs=jax.tree.map(lambda _: VMEM, out_shape),
        out_shape=out_shape,
        scratch_shapes=list(scratch),
        compiler_params=pltpu.CompilerParams(vmem_limit_bytes=vmem * 1024 * 1024),
        cost_estimate=pl.CostEstimate(flops=flops, bytes_accessed=moved, transcendentals=0),
        name=name,
    )


def blk_shift(dz, dx, dc):
    pairs = []
    for s in range(N_BLK):
        z, x, c = s // (X * C), s // C % X, s % C
        pairs.append((s, ((z + dz) % Z * X + (x + dx) % X) * C + (c + dc) % C))
    return pairs


def send(v, *shift):
    return lax.ppermute(v, "blk", blk_shift(*shift))


def near_column(block):
    own = [block, send(block, 1, 0, 0), send(block, -1, 0, 0), send(block, 0, 1, 0)]
    return own + [send(v, 0, 0, 1) for v in own]


def far_column(below, above, across):
    across_below = send(across, 1, 0, 0)
    far = send(above, -1, 0, 0)
    across_above = send(above, 0, 1, 0)
    return across_below, far, across_above


def far_rest(across_below, far, across_above, half):
    own = [
        across_below,
        far,
        across_above,
        send(across_below[:half], 1, 0, 0),
        send(far[half:], 0, 1, 0),
    ]
    return own + [send(v, 0, 0, 1) for v in own]


def places_of(blk):
    z, x, c = blk // (X * C), blk // C % X, blk % C
    shifts = [(0, 0), (-1, 0), (1, 0), (0, 1)], [(-1, 1), (2, 0), (1, 1), (2, 1)]
    return [
        ((z + dz + Z) % Z * X + (x + dx) % X) * C + (c + dc) % C
        for batch in shifts
        for dc in range(C)
        for dz, dx in batch
    ]


def block_kernel(pos_ref, query_ref, out_ref):
    dim = query_ref.shape[1]
    out_ref[:, :dim] = query_ref[...]
    line = lax.broadcasted_iota(jnp.int32, (ROWS, TAIL), 0)
    lane = lax.broadcasted_iota(jnp.int32, (ROWS, TAIL), 1)
    index = jnp.zeros_like(line)
    for r in range(ROWS):
        index = jnp.where(line == r, pos_ref[r], index)
    coded = jnp.where(lane == 0, index // POS_BASE, jnp.where(lane == 1, index % POS_BASE, 0))
    out_ref[:, dim:] = coded.astype(f32).astype(bf16)


def split3(v):
    hi = v.astype(bf16)
    rest = v - hi.astype(f32)
    mid = rest.astype(bf16)
    return hi, mid, (rest - mid.astype(f32)).astype(bf16)


def exact_dot(v, onehot, dims):
    parts = [lax.dot_general(p, onehot, dims, preferred_element_type=f32) for p in split3(v)]
    return parts[0] + parts[1] + parts[2]


def batch_scores(first_slot, blocks, doc_ref, score_ref, query_ref, stat_ref, pos_ref, left_ref, tail_ref):
    half, dim = query_ref.shape
    at = 0
    for block in blocks:
        rows = block.shape[0]
        query_ref[at : at + rows, :] = block[:, :dim]
        tail_ref[at : at + rows, :] = block[:, dim:]
        at += rows
    lane = lax.broadcasted_iota(jnp.int32, (8, TAIL), 1)
    line = lax.broadcasted_iota(jnp.int32, (8, TAIL), 0)
    pick = jnp.where(lane == line, 1.0, 0.0).astype(bf16)
    parts = lax.dot_general(pick, tail_ref[...], contract_last, preferred_element_type=f32)
    positive = (parts[0:1] * POS_BASE + parts[1:2]).astype(jnp.int32) - first_slot
    pos_ref[...] = positive
    steps = doc_ref.shape[0] // TILE

    def multiply(t, top):
        at = pl.multiple_of(t * TILE, TILE)
        scores = sharpness_scale * lax.dot_general(
            doc_ref[pl.ds(at, TILE), :], query_ref[...], contract_last, preferred_element_type=f32
        )
        score_ref[pl.ds(at, TILE), :] = scores
        return jnp.maximum(top, jnp.max(scores, axis=0, keepdims=True))

    top = lax.fori_loop(0, steps, multiply, jnp.full((1, half), -jnp.inf, f32))
    wide = 2 * SUB
    lines = half // ROWS * wide
    line = lax.broadcasted_iota(jnp.int32, (lines, half), 0)
    lane = lax.broadcasted_iota(jnp.int32, (lines, half), 1)
    wanted = jnp.where(lane == line // wide * ROWS + line % SUB, 1.0, 0.0).astype(bf16)
    is_u = lax.broadcasted_iota(jnp.int32, (lines, TILE), 0) % wide < SUB

    def sums(t, carry):
        at = pl.multiple_of(t * TILE, TILE)
        scores = score_ref[pl.ds(at, TILE), :]
        hit = at + lax.broadcasted_iota(jnp.int32, scores.shape, 0) == positive
        exps = jnp.exp(scores - top)
        total = carry[0] + jnp.sum(exps, axis=0, keepdims=True)
        found = carry[1] + jnp.sum(jnp.where(hit, scores, 0.0), axis=0, keepdims=True)
        others = jnp.where(hit, 0.0, exps).astype(bf16)
        onehot = jnp.where(hit, 1.0, 0.0).astype(bf16)
        left_ref[:, pl.ds(at, TILE)] = jnp.where(
            is_u,
            lax.dot_general(wanted, others, contract_last, preferred_element_type=f32),
            lax.dot_general(wanted, onehot, contract_last, preferred_element_type=f32),
        ).astype(bf16)
        return total, found

    zero = jnp.zeros((1, half), f32)
    total, found = lax.fori_loop(0, steps, sums, (zero, zero))
    stat_ref[...] = jnp.concatenate([top, total, found, jnp.zeros((5, half), f32)], axis=0)


def first_kernel(blk_ref, *refs):
    blocks, refs = refs[:-10], refs[-10:]
    hidden_ref, gain_ref, doc_ref, normed_ref = refs[:4]
    hidden = hidden_ref[...].astype(f32)
    inv_rms = lax.rsqrt(jnp.mean(hidden * hidden, axis=1, keepdims=True) + epsilon)
    normed = hidden * inv_rms * gain_ref[...]
    normed_ref[...] = jnp.concatenate([normed, jnp.zeros((8 - SUB, hidden.shape[1]), f32)], axis=0).astype(bf16)
    batch_scores(blk_ref[0] * doc_ref.shape[0], blocks, doc_ref, *refs[4:])


def second_kernel(blk_ref, *refs):
    blocks, refs = refs[:-14], refs[-14:]
    stat_first, left_first, normed_ref, doc_ref, all_ref, sub_ref, order_ref = refs[:7]
    score_ref, query_ref, pos_ref, stat_ref, left_ref, tail_ref, acc = refs[7:]
    cols = order_ref.shape[0]
    lane = lax.broadcasted_iota(jnp.int32, (ROWS, cols), 1)
    line = lax.broadcasted_iota(jnp.int32, (ROWS, cols), 0)
    places = places_of(blk_ref[0])
    for k in range(N_BLK):
        order_ref[k * ROWS : (k + 1) * ROWS, :] = jnp.where(lane == places[k] * ROWS + line, 1.0, 0.0).astype(bf16)
    batch_scores(
        blk_ref[0] * doc_ref.shape[0], blocks, doc_ref, score_ref, query_ref, stat_ref, pos_ref, left_ref, tail_ref
    )
    stats = jnp.concatenate([stat_first[...], stat_ref[...]], axis=1)
    stats = exact_dot(stats, order_ref[...], (((1,), (0,)), ((), ())))
    all_ref[...] = stats
    parts = split3(stats)
    four = 2 * SUB
    lines = N_BLK * WIDE
    line = lax.broadcasted_iota(jnp.int32, (lines, N_BLK * four), 0)
    lane = lax.broadcasted_iota(jnp.int32, (lines, N_BLK * four), 1)
    swap = jnp.zeros(line.shape, f32)
    for k in range(N_BLK):
        swap = jnp.where((lane // four == k) & (line == places[k] * WIDE + lane % four), 1.0, swap)
    left = jnp.concatenate([left_first[...], left_ref[...]], axis=0)
    left = jnp.dot(swap.astype(bf16), left, preferred_element_type=f32).astype(bf16)
    line = lax.broadcasted_iota(jnp.int32, (lines, 8), 0)
    lane = lax.broadcasted_iota(jnp.int32, (lines, 8), 1)
    spread = jnp.where((line % WIDE - four == lane) & (lane < SUB), 1.0, 0.0).astype(bf16)
    acc[...] = jnp.dot(spread, normed_ref[...], preferred_element_type=f32)
    acc[...] += jnp.dot(left, doc_ref[...], preferred_element_type=f32)
    line = lax.broadcasted_iota(jnp.int32, (lines, cols), 0)
    lane = lax.broadcasted_iota(jnp.int32, (lines, cols), 1)
    wanted = jnp.where((lane == line // WIDE * ROWS + line % WIDE) & (line % WIDE < SUB), 1.0, 0.0).astype(bf16)
    stat_rows = [
        lax.dot_general(wanted, p, contract_last, preferred_element_type=f32).astype(bf16) for p in parts
    ]
    width = doc_ref.shape[1] // N_GRP
    grads = acc[...].astype(bf16)
    tail = jnp.concatenate(stat_rows + [jnp.zeros((lines, LANES - width - 24), bf16)], axis=1)
    for g in range(N_GRP):
        sub_ref[g] = jnp.concatenate([grads[:, g * width : (g + 1) * width], tail], axis=1)


def merge_kernel(*refs):
    refs, out_ref = refs[:-1], refs[-1]
    top = functools.reduce(jnp.maximum, [r[0:1] for r in refs])
    total = sum(r[1:2] * jnp.exp(r[0:1] - top) for r in refs)
    found = sum(r[2:3] for r in refs)
    out_ref[...] = jnp.concatenate([top, total, found, jnp.zeros_like(out_ref[3:])], axis=0)


def cotangent_kernel(got_ref, cot_ref):
    width = cot_ref.shape[2]
    rows = got_ref[:, :, : 2 * SUB, :].astype(f32)
    terms, hits, tail = rows[:, :, :SUB, :width], rows[:, :, SUB:, :width], rows[:, :, :SUB, width:]
    stat = lambda k: tail[..., k : k + 1] + tail[..., k + 8 : k + 9] + tail[..., k + 16 : k + 17]
    top = jnp.max(stat(0), axis=1, keepdims=True)
    total = jnp.sum(stat(1) * jnp.exp(stat(0) - top), axis=1, keepdims=True)
    log_total = top + jnp.log(total)
    found = jnp.sum(stat(2), axis=1, keepdims=True)
    scale = jnp.exp(stat(0) - log_total)
    grads = jnp.sum(scale * terms + (jnp.exp(found - log_total) - 1.0) * hits, axis=1)
    grads = sharpness_scale * grads
    grads = jnp.concatenate([grads[g] for g in range(N_GRP)], axis=0).astype(bf16)
    for b in range(N_BLK):
        cot_ref[b] = grads


def weight_kernel(grp_ref, stats_ref, pos_a, pos_b, order_ref, first_ref, second_ref, query_a, query_b, *refs):
    loss_ref, whole_ref, own_ref, other_ref, total = refs
    step = pl.program_id(0)
    cols = order_ref.shape[1]
    half = cols // 2

    @pl.when(step == 0)
    def _():
        log_total = stats_ref[0:1] + jnp.log(stats_ref[1:2])
        losses = log_total - stats_ref[2:3]
        both = jnp.concatenate([log_total, losses, jnp.zeros((6, cols), f32)], axis=0)
        both = exact_dot(both, order_ref[...], contract_last)
        loss_ref[...] = both[1:2]
        total[...] = both[0:1]

    rows = first_ref.shape[2]
    out = None
    for k, (score_ref, query_ref, pos_ref) in enumerate(
        ((first_ref, query_a, pos_a), (second_ref, query_b, pos_b))
    ):
        scores = score_ref[...].reshape(GX * rows, half)
        line = lax.broadcasted_iota(jnp.int32, scores.shape, 0)
        slot = (line // rows * GY + step) * rows + line % rows
        onehot = jnp.where(slot == pos_ref[...], 1.0, 0.0)
        weights = (jnp.exp(scores - total[:, k * half : (k + 1) * half]) - onehot).astype(bf16)
        term = jnp.dot(weights, query_ref[...], preferred_element_type=f32)
        out = term if out is None else out + term
    out = sharpness_scale * out
    first_x = grp_ref[0] // GY == 0
    whole_ref[...] = out[:, :Y_FIRST].astype(bf16)
    own_ref[...] = jnp.where(first_x, out[:rows, Y_FIRST:], out[rows:, Y_FIRST:]).astype(bf16)
    other_ref[...] = jnp.where(first_x, out[rows:, Y_FIRST:], out[:rows, Y_FIRST:]).astype(bf16)


def passage_terms(grp, stats, pos_a, pos_b, order, score_a, score_b, query_a, query_b):
    shard_rows, half = score_a.shape
    dim = query_a.shape[1]
    rows = shard_rows // N_GRP
    shape = jax.ShapeDtypeStruct
    fixed = lambda v: pl.BlockSpec(v.shape, lambda i: (0,) * len(v.shape))
    scores = pl.BlockSpec((GX, 1, rows, half), lambda i: (0, i, 0, 0))
    apart = pl.BlockSpec((rows, dim - Y_FIRST), lambda i: (i, 0))
    loss = shape((1, 2 * half), f32)
    return pl.pallas_call(
        weight_kernel,
        grid=(GY,),
        in_specs=[SMEM, fixed(stats), fixed(pos_a), fixed(pos_b), fixed(order), scores, scores]
        + [fixed(query_a), fixed(query_b)],
        out_specs=[fixed(loss), pl.BlockSpec((GX * rows, Y_FIRST), lambda i: (i, 0)), apart, apart],
        out_shape=[loss, shape((shard_rows, Y_FIRST), bf16)]
        + [shape((GY * rows, dim - Y_FIRST), bf16)] * 2,
        scratch_shapes=[pltpu.VMEM((1, 2 * half), f32)],
        compiler_params=pltpu.CompilerParams(vmem_limit_bytes=52 * 1024 * 1024),
        cost_estimate=pl.CostEstimate(
            flops=4 * shard_rows * half * dim, bytes_accessed=4 * shard_rows * dim, transcendentals=0
        ),
        name="passage_terms",
    )(
        grp,
        stats,
        pos_a,
        pos_b,
        order,
        score_a.reshape(GX, GY, rows, half),
        score_b.reshape(GX, GY, rows, half),
        query_a,
        query_b,
    )


def x_sum_kernel(own_ref, got_ref, out_ref):
    out_ref[...] = (own_ref[...].astype(f32) + got_ref[...].astype(f32)).astype(bf16)


def x_split_kernel(grp_ref, both_ref, own_ref, other_ref):
    rows = own_ref.shape[0]
    first_x = grp_ref[0] // GY == 0
    above, below = both_ref[:rows].astype(f32), both_ref[rows:].astype(f32)
    own_ref[...] = jnp.where(first_x, above, below).astype(bf16)
    other_ref[...] = jnp.where(first_x, below, above).astype(bf16)


def passage_kernel(own_ref, got_ref, rest_ref, out_ref):
    out_ref[:, :Y_FIRST] = own_ref[...].astype(f32) + got_ref[...].astype(f32)
    out_ref[:, Y_FIRST:] = rest_ref[...].astype(f32)


def send_x(v):
    return lax.ppermute(v, "grp", [(g, (g + GY) % N_GRP) for g in range(N_GRP)])


def y_sum(v):
    return lax.psum_scatter(v, "grp", scatter_dimension=0, axis_index_groups=Y_GROUPS, tiled=True)


def act_kernel(blk_ref, cot_ref, got_ref, down_ref, gate_ref, up_ref, out_ref, normed):
    part, units = down_ref.shape
    for g in range(N_GRP):
        for b in range(N_BLK):
            at = (g * N_BLK + b) * SUB
            normed[at : at + SUB, :] = got_ref[g, b, 2 * SUB :, :part].astype(f32)
    rows = cot_ref[...].reshape(-1, part)
    count = rows.shape[0]
    line = lax.broadcasted_iota(jnp.int32, (count, count), 0)
    lane = lax.broadcasted_iota(jnp.int32, (count, count), 1)
    per = N_BLK * SUB
    swap = jnp.where(lane == (line % per // SUB * N_GRP + line // per) * SUB + line % SUB, 1.0, 0.0).astype(bf16)
    rows = jnp.dot(swap, rows, preferred_element_type=f32).astype(bf16)
    values = [jnp.dot(rows, down_ref[...], preferred_element_type=f32).astype(bf16)]
    rows = normed[...].astype(bf16)
    values.append(jnp.dot(rows, gate_ref[...], preferred_element_type=f32).astype(bf16))
    values.append(jnp.dot(rows, up_ref[...], preferred_element_type=f32).astype(bf16))
    own = cot_ref[blk_ref[0]]
    width = part // N_GRP
    blank = jnp.zeros((per - N_GRP * SUB, width), bf16)
    for g in range(N_GRP):
        mine = own[g * SUB : (g + 1) * SUB].astype(f32)
        pieces = [mine[:, k * width : (k + 1) * width] for k in range(N_GRP)]
        pieces = jnp.concatenate(pieces, axis=0).astype(bf16)
        for k in range(3):
            out_ref[g, k * per : (k + 1) * per, :units] = values[k][g * per : (g + 1) * per]
        out_ref[g, :per, units : units + width] = jnp.concatenate([pieces, blank], axis=0)
        out_ref[g, per:, units : units + width] = jnp.zeros((2 * per, width), bf16)


def swiglu_kernel(got_ref, out_ref, cot_ref):
    per = got_ref.shape[1] // 3
    units = out_ref.shape[2]
    sums = jnp.sum(got_ref[:, :, :units].astype(f32), axis=0)
    act_grad, gate_value, up_value = sums[:per], sums[per : 2 * per], sums[2 * per :]
    gate_sigmoid = jax.nn.sigmoid(gate_value)
    up_grad = (act_grad * gate_value * gate_sigmoid).astype(bf16)
    gate_grad = (act_grad * up_value * gate_sigmoid * (1.0 + gate_value * (1.0 - gate_sigmoid))).astype(bf16)
    for g in range(N_GRP):
        out_ref[g, :per] = gate_grad
        out_ref[g, per:] = up_grad
    pieces = got_ref[:, : N_GRP * SUB, units:].astype(f32)
    cot_ref[...] = jnp.concatenate(
        [pieces[g, k * SUB : (k + 1) * SUB] for g in range(N_GRP) for k in range(N_GRP)], axis=1
    )


def backward_kernel(grad_ref, gate_ref, up_ref, out_ref):
    per = grad_ref.shape[1] // 2
    both = grad_ref[...]
    gate_grad = both[:, :per].reshape(N_GRP * per, -1)
    up_grad = both[:, per:].reshape(N_GRP * per, -1)
    total = lax.dot_general(gate_grad, gate_ref[...], contract_last, preferred_element_type=f32)
    total += lax.dot_general(up_grad, up_ref[...], contract_last, preferred_element_type=f32)
    for g in range(N_GRP):
        out_ref[g] = total[g * per : (g + 1) * per].astype(bf16)


def hidden_kernel(back_ref, cot_ref, hidden_ref, gain_ref, out_ref):
    sums = jnp.sum(back_ref[...].astype(f32), axis=1)
    normed_grad = jnp.concatenate([sums[g] for g in range(N_GRP)], axis=1)
    hidden = hidden_ref[...].astype(f32)
    inv_rms = lax.rsqrt(jnp.mean(hidden * hidden, axis=1, keepdims=True) + epsilon)
    scaled = normed_grad * gain_ref[...]
    mean = jnp.mean(hidden * scaled, axis=1, keepdims=True)
    out_ref[...] = cot_ref[...] + inv_rms * scaled - hidden * inv_rms * inv_rms * inv_rms * mean


def exchange(v, axis):
    return lax.all_to_all(v, axis, 0, 0, tiled=True)


def shards(
    queries, stored_documents, positive, last_hidden, norm_gain, gate_weight, up_weight, down_weight
):
    shape = jax.ShapeDtypeStruct
    blk = lax.axis_index("blk").astype(jnp.int32)[None]
    grp = lax.axis_index("grp").astype(jnp.int32)[None]
    shard_rows, dim = stored_documents.shape
    part = dim // N_GRP
    units = gate_weight.shape[1]
    cols = N_BLK * ROWS
    half = cols // 2
    per = N_BLK * SUB
    gain = norm_gain[None]

    block = local(block_kernel, "block", shape((ROWS, dim + TAIL), bf16), scalars=1, count=1)(
        positive, queries
    )
    first = near_column(block)
    second = far_column(*first[1:4])

    product = 2 * shard_rows * half * dim
    normed, score_a, query_a, stat_a, pos_a, left_a = local(
        first_kernel,
        "first_scores",
        [
            shape((8, dim), bf16),
            shape((shard_rows, half), f32),
            shape((half, dim), bf16),
            shape((8, half), f32),
            shape((1, half), jnp.int32),
            shape((per, shard_rows), bf16),
        ],
        scratch=[pltpu.VMEM((half, TAIL), bf16)],
        scalars=1,
        count=len(first) + 3,
        flops=2 * product,
        moved=4 * shard_rows * dim,
    )(blk, *first, last_hidden, gain, stored_documents)
    second, left_a = lax.optimization_barrier((second, left_a))
    second = far_rest(*second, ROWS // 2)
    stats, sub_terms, order, score_b, query_b, pos_b = local(
        second_kernel,
        "second_scores",
        [
            shape((8, cols), f32),
            shape((N_GRP, N_BLK * WIDE, LANES), bf16),
            shape((cols, cols), bf16),
            shape((shard_rows, half), f32),
            shape((half, dim), bf16),
            shape((1, half), jnp.int32),
        ],
        scratch=[
            pltpu.VMEM((8, half), f32),
            pltpu.VMEM((per, shard_rows), bf16),
            pltpu.VMEM((half, TAIL), bf16),
            pltpu.VMEM((N_BLK * WIDE, dim), f32),
        ],
        scalars=1,
        count=len(second) + 4,
        flops=2 * product,
        moved=4 * shard_rows * dim,
    )(blk, *second, stat_a, left_a, normed, stored_documents)

    got = exchange(sub_terms.reshape(N_GRP * N_BLK, WIDE, LANES), ("grp", "blk"))
    for steps in ([(0, 1, 0), (0, 0, 1), (0, 1, 1)], [(1, 0, 0), (2, 0, 0), (3, 0, 0)]):
        stats = local(merge_kernel, "merge", shape((8, cols), f32), count=4)(
            stats, *[send(stats, *step) for step in steps]
        )
    loss_row, whole, own, other = passage_terms(
        grp, stats, pos_a, pos_b, order, score_a, score_b, query_a, query_b
    )
    losses = loss_row[0, :ROWS]
    got = got.reshape(N_GRP, N_BLK, WIDE, LANES)
    cot = local(cotangent_kernel, "cotangents", shape((N_BLK, N_GRP * SUB, part), bf16), count=1)(got)
    cot, whole, other = lax.optimization_barrier((cot, whole, other))
    other = send_x(other)
    whole = y_sum(whole)
    cot = exchange(cot, "blk")

    values = local(
        act_kernel,
        "act",
        shape((N_GRP, 3 * per, units + part // N_GRP), bf16),
        scratch=[pltpu.VMEM((N_GRP * per, part), f32)],
        scalars=1,
        count=5,
    )(blk, cot, got, down_weight.T, gate_weight, up_weight)
    grads, cotangent = local(
        swiglu_kernel,
        "swiglu",
        [shape((N_GRP, 2 * per, units), bf16), shape((SUB, dim), f32)],
        count=1,
    )(exchange(values, "grp"))
    grads, other = lax.optimization_barrier((grads, other))
    rest = local(x_sum_kernel, "x_sum", shape(own.shape, bf16), count=2)(own, other)
    grads, rest = lax.optimization_barrier((grads, rest))
    rest = y_sum(rest)
    normed_part = local(backward_kernel, "backward", shape((N_GRP, per, part), bf16), count=3)(
        exchange(grads, "grp"), gate_weight, up_weight
    )
    normed_part, whole = lax.optimization_barrier((normed_part, whole))
    own, other = local(
        x_split_kernel, "x_split", [shape((shard_rows // N_GRP, Y_FIRST), bf16)] * 2, scalars=1, count=1
    )(grp, whole)
    normed_part, other = lax.optimization_barrier((normed_part, other))
    other = send_x(other)
    back = exchange(normed_part.reshape(N_GRP * N_BLK, SUB, part), ("grp", "blk"))
    passage_grads = local(passage_kernel, "passages", shape((shard_rows // N_GRP, dim), f32), count=3)(
        own, other, rest
    )
    hidden_grads = local(hidden_kernel, "hidden", shape((SUB, dim), f32), count=4)(
        back.reshape(N_GRP, N_BLK, SUB, part), cotangent, last_hidden, gain
    )
    return (losses, passage_grads, hidden_grads)


def solution(mesh):
    return jax.shard_map(
        shards,
        mesh=mesh,
        in_specs=(
            P(("blk", "grp"), None),
            P("blk", None),
            P(("blk", "grp")),
            P(("blk", "grp"), None),
            P(),
            P("grp", "blk"),
            P("grp", "blk"),
            P("blk", "grp"),
        ),
        out_specs=(P(("blk", "grp")), P(("blk", "grp"), None), P(("blk", "grp"), None)),
        check_vma=False,
    )
```

```python
import functools

import jax
import jax.numpy as jnp
from jax import lax
from jax.experimental import pallas as pl
from jax.experimental.pallas import tpu as pltpu
from jax.sharding import PartitionSpec as P

sharpness_scale = 20.0
epsilon = 1e-06
contract_last = (((1,), (1,)), ((), ()))
Z, X, C = 4, 2, 2
N_BLK, N_GRP = 16, 8
POS_BASE = 128
TAIL = 128
ROWS = 32
SUB = 2
WIDE = 3 * SUB
LANES = 512
Y_FIRST = 2688
GX, GY = 2, 4
Y_GROUPS = [[x * GY + y for y in range(GY)] for x in range(GX)]
TILE = 256
f32, bf16 = jnp.float32, jnp.bfloat16
VMEM = pl.BlockSpec(memory_space=pltpu.VMEM)
SMEM = pl.BlockSpec(memory_space=pltpu.SMEM)


def local(kernel, name, out_shape, scratch=(), scalars=0, count=0, flops=0, moved=0, vmem=32):
    return pl.pallas_call(
        kernel,
        in_specs=[SMEM] * scalars + [VMEM] * count,
        out_specs=jax.tree.map(lambda _: VMEM, out_shape),
        out_shape=out_shape,
        scratch_shapes=list(scratch),
        compiler_params=pltpu.CompilerParams(vmem_limit_bytes=vmem * 1024 * 1024),
        cost_estimate=pl.CostEstimate(flops=flops, bytes_accessed=moved, transcendentals=0),
        name=name,
    )


def blk_shift(dz, dx, dc):
    pairs = []
    for s in range(N_BLK):
        z, x, c = s // (X * C), s // C % X, s % C
        pairs.append((s, ((z + dz) % Z * X + (x + dx) % X) * C + (c + dc) % C))
    return pairs


def send(v, *shift):
    return lax.ppermute(v, "blk", blk_shift(*shift))


def near_column(block):
    own = [block, send(block, 1, 0, 0), send(block, -1, 0, 0), send(block, 0, 1, 0)]
    return own + [send(v, 0, 0, 1) for v in own]


def far_column(below, above, across):
    across_below = send(across, 1, 0, 0)
    far = send(above, -1, 0, 0)
    across_above = send(above, 0, 1, 0)
    return across_below, far, across_above


def far_rest(across_below, far, across_above, half):
    own = [
        across_below,
        far,
        across_above,
        send(across_below[:half], 1, 0, 0),
        send(far[half:], 0, 1, 0),
    ]
    return own + [send(v, 0, 0, 1) for v in own]


def places_of(blk):
    z, x, c = blk // (X * C), blk // C % X, blk % C
    shifts = [(0, 0), (-1, 0), (1, 0), (0, 1)], [(-1, 1), (2, 0), (1, 1), (2, 1)]
    return [
        ((z + dz + Z) % Z * X + (x + dx) % X) * C + (c + dc) % C
        for batch in shifts
        for dc in range(C)
        for dz, dx in batch
    ]


def block_kernel(pos_ref, query_ref, out_ref):
    dim = query_ref.shape[1]
    out_ref[:, :dim] = query_ref[...]
    line = lax.broadcasted_iota(jnp.int32, (ROWS, TAIL), 0)
    lane = lax.broadcasted_iota(jnp.int32, (ROWS, TAIL), 1)
    index = jnp.zeros_like(line)
    for r in range(ROWS):
        index = jnp.where(line == r, pos_ref[r], index)
    coded = jnp.where(lane == 0, index // POS_BASE, jnp.where(lane == 1, index % POS_BASE, 0))
    out_ref[:, dim:] = coded.astype(f32).astype(bf16)


def split3(v):
    hi = v.astype(bf16)
    rest = v - hi.astype(f32)
    mid = rest.astype(bf16)
    return hi, mid, (rest - mid.astype(f32)).astype(bf16)


def exact_dot(v, onehot, dims):
    parts = [lax.dot_general(p, onehot, dims, preferred_element_type=f32) for p in split3(v)]
    return parts[0] + parts[1] + parts[2]


def batch_scores(first_slot, blocks, doc_ref, score_ref, query_ref, stat_ref, pos_ref, left_ref, tail_ref):
    half, dim = query_ref.shape
    at = 0
    for block in blocks:
        rows = block.shape[0]
        query_ref[at : at + rows, :] = block[:, :dim]
        tail_ref[at : at + rows, :] = block[:, dim:]
        at += rows
    lane = lax.broadcasted_iota(jnp.int32, (8, TAIL), 1)
    line = lax.broadcasted_iota(jnp.int32, (8, TAIL), 0)
    pick = jnp.where(lane == line, 1.0, 0.0).astype(bf16)
    parts = lax.dot_general(pick, tail_ref[...], contract_last, preferred_element_type=f32)
    positive = (parts[0:1] * POS_BASE + parts[1:2]).astype(jnp.int32) - first_slot
    pos_ref[...] = positive
    steps = doc_ref.shape[0] // TILE

    def multiply(t, top):
        at = pl.multiple_of(t * TILE, TILE)
        scores = sharpness_scale * lax.dot_general(
            doc_ref[pl.ds(at, TILE), :], query_ref[...], contract_last, preferred_element_type=f32
        )
        score_ref[pl.ds(at, TILE), :] = scores
        return jnp.maximum(top, jnp.max(scores, axis=0, keepdims=True))

    top = lax.fori_loop(0, steps, multiply, jnp.full((1, half), -jnp.inf, f32))
    wide = 2 * SUB
    lines = half // ROWS * wide
    line = lax.broadcasted_iota(jnp.int32, (lines, half), 0)
    lane = lax.broadcasted_iota(jnp.int32, (lines, half), 1)
    wanted = jnp.where(lane == line // wide * ROWS + line % SUB, 1.0, 0.0).astype(bf16)
    is_u = lax.broadcasted_iota(jnp.int32, (lines, TILE), 0) % wide < SUB

    def sums(t, carry):
        at = pl.multiple_of(t * TILE, TILE)
        scores = score_ref[pl.ds(at, TILE), :]
        hit = at + lax.broadcasted_iota(jnp.int32, scores.shape, 0) == positive
        exps = jnp.exp(scores - top)
        total = carry[0] + jnp.sum(exps, axis=0, keepdims=True)
        found = carry[1] + jnp.sum(jnp.where(hit, scores, 0.0), axis=0, keepdims=True)
        others = jnp.where(hit, 0.0, exps).astype(bf16)
        onehot = jnp.where(hit, 1.0, 0.0).astype(bf16)
        left_ref[:, pl.ds(at, TILE)] = jnp.where(
            is_u,
            lax.dot_general(wanted, others, contract_last, preferred_element_type=f32),
            lax.dot_general(wanted, onehot, contract_last, preferred_element_type=f32),
        ).astype(bf16)
        return total, found

    zero = jnp.zeros((1, half), f32)
    total, found = lax.fori_loop(0, steps, sums, (zero, zero))
    stat_ref[...] = jnp.concatenate([top, total, found, jnp.zeros((5, half), f32)], axis=0)


def first_kernel(blk_ref, *refs):
    blocks, refs = refs[:-10], refs[-10:]
    hidden_ref, gain_ref, doc_ref, normed_ref = refs[:4]
    hidden = hidden_ref[...].astype(f32)
    inv_rms = lax.rsqrt(jnp.mean(hidden * hidden, axis=1, keepdims=True) + epsilon)
    normed = hidden * inv_rms * gain_ref[...]
    normed_ref[...] = jnp.concatenate([normed, jnp.zeros((8 - SUB, hidden.shape[1]), f32)], axis=0).astype(bf16)
    batch_scores(blk_ref[0] * doc_ref.shape[0], blocks, doc_ref, *refs[4:])


def second_kernel(blk_ref, *refs):
    blocks, refs = refs[:-14], refs[-14:]
    stat_first, left_first, normed_ref, doc_ref, all_ref, sub_ref, order_ref = refs[:7]
    score_ref, query_ref, pos_ref, stat_ref, left_ref, tail_ref, acc = refs[7:]
    cols = order_ref.shape[0]
    lane = lax.broadcasted_iota(jnp.int32, (ROWS, cols), 1)
    line = lax.broadcasted_iota(jnp.int32, (ROWS, cols), 0)
    places = places_of(blk_ref[0])
    for k in range(N_BLK):
        order_ref[k * ROWS : (k + 1) * ROWS, :] = jnp.where(lane == places[k] * ROWS + line, 1.0, 0.0).astype(bf16)
    batch_scores(
        blk_ref[0] * doc_ref.shape[0], blocks, doc_ref, score_ref, query_ref, stat_ref, pos_ref, left_ref, tail_ref
    )
    stats = jnp.concatenate([stat_first[...], stat_ref[...]], axis=1)
    stats = exact_dot(stats, order_ref[...], (((1,), (0,)), ((), ())))
    all_ref[...] = stats
    parts = split3(stats)
    four = 2 * SUB
    lines = N_BLK * WIDE
    line = lax.broadcasted_iota(jnp.int32, (lines, N_BLK * four), 0)
    lane = lax.broadcasted_iota(jnp.int32, (lines, N_BLK * four), 1)
    swap = jnp.zeros(line.shape, f32)
    for k in range(N_BLK):
        swap = jnp.where((lane // four == k) & (line == places[k] * WIDE + lane % four), 1.0, swap)
    left = jnp.concatenate([left_first[...], left_ref[...]], axis=0)
    left = jnp.dot(swap.astype(bf16), left, preferred_element_type=f32).astype(bf16)
    line = lax.broadcasted_iota(jnp.int32, (lines, 8), 0)
    lane = lax.broadcasted_iota(jnp.int32, (lines, 8), 1)
    spread = jnp.where((line % WIDE - four == lane) & (lane < SUB), 1.0, 0.0).astype(bf16)
    acc[...] = jnp.dot(spread, normed_ref[...], preferred_element_type=f32)
    acc[...] += jnp.dot(left, doc_ref[...], preferred_element_type=f32)
    line = lax.broadcasted_iota(jnp.int32, (lines, cols), 0)
    lane = lax.broadcasted_iota(jnp.int32, (lines, cols), 1)
    wanted = jnp.where((lane == line // WIDE * ROWS + line % WIDE) & (line % WIDE < SUB), 1.0, 0.0).astype(bf16)
    stat_rows = [
        lax.dot_general(wanted, p, contract_last, preferred_element_type=f32).astype(bf16) for p in parts
    ]
    width = doc_ref.shape[1] // N_GRP
    grads = acc[...].astype(bf16)
    tail = jnp.concatenate(stat_rows + [jnp.zeros((lines, LANES - width - 24), bf16)], axis=1)
    for g in range(N_GRP):
        sub_ref[g] = jnp.concatenate([grads[:, g * width : (g + 1) * width], tail], axis=1)


def merge_kernel(*refs):
    refs, out_ref = refs[:-1], refs[-1]
    top = functools.reduce(jnp.maximum, [r[0:1] for r in refs])
    total = sum(r[1:2] * jnp.exp(r[0:1] - top) for r in refs)
    found = sum(r[2:3] for r in refs)
    out_ref[...] = jnp.concatenate([top, total, found, jnp.zeros_like(out_ref[3:])], axis=0)


def cotangent_kernel(got_ref, cot_ref):
    width = cot_ref.shape[2]
    rows = got_ref[:, :, : 2 * SUB, :].astype(f32)
    terms, hits, tail = rows[:, :, :SUB, :width], rows[:, :, SUB:, :width], rows[:, :, :SUB, width:]
    stat = lambda k: tail[..., k : k + 1] + tail[..., k + 8 : k + 9] + tail[..., k + 16 : k + 17]
    top = jnp.max(stat(0), axis=1, keepdims=True)
    total = jnp.sum(stat(1) * jnp.exp(stat(0) - top), axis=1, keepdims=True)
    log_total = top + jnp.log(total)
    found = jnp.sum(stat(2), axis=1, keepdims=True)
    scale = jnp.exp(stat(0) - log_total)
    grads = jnp.sum(scale * terms + (jnp.exp(found - log_total) - 1.0) * hits, axis=1)
    grads = sharpness_scale * grads
    grads = jnp.concatenate([grads[g] for g in range(N_GRP)], axis=0).astype(bf16)
    for b in range(N_BLK):
        cot_ref[b] = grads


def weight_kernel(grp_ref, stats_ref, pos_a, pos_b, order_ref, first_ref, second_ref, query_a, query_b, *refs):
    loss_ref, whole_ref, own_ref, other_ref, total = refs
    step = pl.program_id(0)
    cols = order_ref.shape[1]
    half = cols // 2

    @pl.when(step == 0)
    def _():
        log_total = stats_ref[0:1] + jnp.log(stats_ref[1:2])
        losses = log_total - stats_ref[2:3]
        both = jnp.concatenate([log_total, losses, jnp.zeros((6, cols), f32)], axis=0)
        both = exact_dot(both, order_ref[...], contract_last)
        loss_ref[...] = both[1:2]
        total[...] = both[0:1]

    rows = first_ref.shape[2]
    out = None
    for k, (score_ref, query_ref, pos_ref) in enumerate(
        ((first_ref, query_a, pos_a), (second_ref, query_b, pos_b))
    ):
        scores = score_ref[...].reshape(GX * rows, half)
        line = lax.broadcasted_iota(jnp.int32, scores.shape, 0)
        slot = (line // rows * GY + step) * rows + line % rows
        onehot = jnp.where(slot == pos_ref[...], 1.0, 0.0)
        weights = (jnp.exp(scores - total[:, k * half : (k + 1) * half]) - onehot).astype(bf16)
        term = jnp.dot(weights, query_ref[...], preferred_element_type=f32)
        out = term if out is None else out + term
    out = sharpness_scale * out
    first_x = grp_ref[0] // GY == 0
    whole_ref[...] = out[:, :Y_FIRST].astype(bf16)
    own_ref[...] = jnp.where(first_x, out[:rows, Y_FIRST:], out[rows:, Y_FIRST:]).astype(bf16)
    other_ref[...] = jnp.where(first_x, out[rows:, Y_FIRST:], out[:rows, Y_FIRST:]).astype(bf16)


def passage_terms(grp, stats, pos_a, pos_b, order, score_a, score_b, query_a, query_b):
    shard_rows, half = score_a.shape
    dim = query_a.shape[1]
    rows = shard_rows // N_GRP
    shape = jax.ShapeDtypeStruct
    fixed = lambda v: pl.BlockSpec(v.shape, lambda i: (0,) * len(v.shape))
    scores = pl.BlockSpec((GX, 1, rows, half), lambda i: (0, i, 0, 0))
    apart = pl.BlockSpec((rows, dim - Y_FIRST), lambda i: (i, 0))
    loss = shape((1, 2 * half), f32)
    return pl.pallas_call(
        weight_kernel,
        grid=(GY,),
        in_specs=[SMEM, fixed(stats), fixed(pos_a), fixed(pos_b), fixed(order), scores, scores]
        + [fixed(query_a), fixed(query_b)],
        out_specs=[fixed(loss), pl.BlockSpec((GX * rows, Y_FIRST), lambda i: (i, 0)), apart, apart],
        out_shape=[loss, shape((shard_rows, Y_FIRST), bf16)]
        + [shape((GY * rows, dim - Y_FIRST), bf16)] * 2,
        scratch_shapes=[pltpu.VMEM((1, 2 * half), f32)],
        compiler_params=pltpu.CompilerParams(vmem_limit_bytes=28 * 1024 * 1024),
        cost_estimate=pl.CostEstimate(
            flops=4 * shard_rows * half * dim, bytes_accessed=4 * shard_rows * dim, transcendentals=0
        ),
        name="passage_terms",
    )(
        grp,
        stats,
        pos_a,
        pos_b,
        order,
        score_a.reshape(GX, GY, rows, half),
        score_b.reshape(GX, GY, rows, half),
        query_a,
        query_b,
    )


def x_sum_kernel(own_ref, got_ref, out_ref):
    out_ref[...] = (own_ref[...].astype(f32) + got_ref[...].astype(f32)).astype(bf16)


def x_split_kernel(grp_ref, both_ref, own_ref, other_ref):
    rows = own_ref.shape[0]
    first_x = grp_ref[0] // GY == 0
    above, below = both_ref[:rows].astype(f32), both_ref[rows:].astype(f32)
    own_ref[...] = jnp.where(first_x, above, below).astype(bf16)
    other_ref[...] = jnp.where(first_x, below, above).astype(bf16)


def passage_kernel(own_ref, got_ref, rest_ref, out_ref):
    out_ref[:, :Y_FIRST] = own_ref[...].astype(f32) + got_ref[...].astype(f32)
    out_ref[:, Y_FIRST:] = rest_ref[...].astype(f32)


def send_x(v):
    return lax.ppermute(v, "grp", [(g, (g + GY) % N_GRP) for g in range(N_GRP)])


def y_sum(v):
    return lax.psum_scatter(v, "grp", scatter_dimension=0, axis_index_groups=Y_GROUPS, tiled=True)


def act_kernel(blk_ref, cot_ref, got_ref, down_ref, gate_ref, up_ref, out_ref, normed):
    part, units = down_ref.shape
    for g in range(N_GRP):
        for b in range(N_BLK):
            at = (g * N_BLK + b) * SUB
            normed[at : at + SUB, :] = got_ref[g, b, 2 * SUB :, :part].astype(f32)
    rows = cot_ref[...].reshape(-1, part)
    count = rows.shape[0]
    line = lax.broadcasted_iota(jnp.int32, (count, count), 0)
    lane = lax.broadcasted_iota(jnp.int32, (count, count), 1)
    per = N_BLK * SUB
    swap = jnp.where(lane == (line % per // SUB * N_GRP + line // per) * SUB + line % SUB, 1.0, 0.0).astype(bf16)
    rows = jnp.dot(swap, rows, preferred_element_type=f32).astype(bf16)
    values = [jnp.dot(rows, down_ref[...], preferred_element_type=f32).astype(bf16)]
    rows = normed[...].astype(bf16)
    values.append(jnp.dot(rows, gate_ref[...], preferred_element_type=f32).astype(bf16))
    values.append(jnp.dot(rows, up_ref[...], preferred_element_type=f32).astype(bf16))
    own = cot_ref[blk_ref[0]]
    width = part // N_GRP
    blank = jnp.zeros((per - N_GRP * SUB, width), bf16)
    for g in range(N_GRP):
        mine = own[g * SUB : (g + 1) * SUB].astype(f32)
        pieces = [mine[:, k * width : (k + 1) * width] for k in range(N_GRP)]
        pieces = jnp.concatenate(pieces, axis=0).astype(bf16)
        for k in range(3):
            out_ref[g, k * per : (k + 1) * per, :units] = values[k][g * per : (g + 1) * per]
        out_ref[g, :per, units : units + width] = jnp.concatenate([pieces, blank], axis=0)
        out_ref[g, per:, units : units + width] = jnp.zeros((2 * per, width), bf16)


def swiglu_kernel(got_ref, out_ref, cot_ref):
    per = got_ref.shape[1] // 3
    units = out_ref.shape[2]
    sums = jnp.sum(got_ref[:, :, :units].astype(f32), axis=0)
    act_grad, gate_value, up_value = sums[:per], sums[per : 2 * per], sums[2 * per :]
    gate_sigmoid = jax.nn.sigmoid(gate_value)
    up_grad = (act_grad * gate_value * gate_sigmoid).astype(bf16)
    gate_grad = (act_grad * up_value * gate_sigmoid * (1.0 + gate_value * (1.0 - gate_sigmoid))).astype(bf16)
    for g in range(N_GRP):
        out_ref[g, :per] = gate_grad
        out_ref[g, per:] = up_grad
    pieces = got_ref[:, : N_GRP * SUB, units:].astype(f32)
    cot_ref[...] = jnp.concatenate(
        [pieces[g, k * SUB : (k + 1) * SUB] for g in range(N_GRP) for k in range(N_GRP)], axis=1
    )


def backward_kernel(grad_ref, gate_ref, up_ref, out_ref):
    per = grad_ref.shape[1] // 2
    both = grad_ref[...]
    gate_grad = both[:, :per].reshape(N_GRP * per, -1)
    up_grad = both[:, per:].reshape(N_GRP * per, -1)
    total = lax.dot_general(gate_grad, gate_ref[...], contract_last, preferred_element_type=f32)
    total += lax.dot_general(up_grad, up_ref[...], contract_last, preferred_element_type=f32)
    for g in range(N_GRP):
        out_ref[g] = total[g * per : (g + 1) * per].astype(bf16)


def hidden_kernel(back_ref, cot_ref, hidden_ref, gain_ref, out_ref):
    sums = jnp.sum(back_ref[...].astype(f32), axis=1)
    normed_grad = jnp.concatenate([sums[g] for g in range(N_GRP)], axis=1)
    hidden = hidden_ref[...].astype(f32)
    inv_rms = lax.rsqrt(jnp.mean(hidden * hidden, axis=1, keepdims=True) + epsilon)
    scaled = normed_grad * gain_ref[...]
    mean = jnp.mean(hidden * scaled, axis=1, keepdims=True)
    out_ref[...] = cot_ref[...] + inv_rms * scaled - hidden * inv_rms * inv_rms * inv_rms * mean


def exchange(v, axis):
    return lax.all_to_all(v, axis, 0, 0, tiled=True)


def shards(
    queries, stored_documents, positive, last_hidden, norm_gain, gate_weight, up_weight, down_weight
):
    shape = jax.ShapeDtypeStruct
    blk = lax.axis_index("blk").astype(jnp.int32)[None]
    grp = lax.axis_index("grp").astype(jnp.int32)[None]
    shard_rows, dim = stored_documents.shape
    part = dim // N_GRP
    units = gate_weight.shape[1]
    cols = N_BLK * ROWS
    half = cols // 2
    per = N_BLK * SUB
    gain = norm_gain[None]

    block = local(block_kernel, "block", shape((ROWS, dim + TAIL), bf16), scalars=1, count=1)(
        positive, queries
    )
    first = near_column(block)
    second = far_column(*first[1:4])

    product = 2 * shard_rows * half * dim
    normed, score_a, query_a, stat_a, pos_a, left_a = local(
        first_kernel,
        "first_scores",
        [
            shape((8, dim), bf16),
            shape((shard_rows, half), f32),
            shape((half, dim), bf16),
            shape((8, half), f32),
            shape((1, half), jnp.int32),
            shape((per, shard_rows), bf16),
        ],
        scratch=[pltpu.VMEM((half, TAIL), bf16)],
        scalars=1,
        count=len(first) + 3,
        flops=2 * product,
        moved=4 * shard_rows * dim,
    )(blk, *first, last_hidden, gain, stored_documents)
    second, left_a = lax.optimization_barrier((second, left_a))
    second = far_rest(*second, ROWS // 2)
    stats, sub_terms, order, score_b, query_b, pos_b = local(
        second_kernel,
        "second_scores",
        [
            shape((8, cols), f32),
            shape((N_GRP, N_BLK * WIDE, LANES), bf16),
            shape((cols, cols), bf16),
            shape((shard_rows, half), f32),
            shape((half, dim), bf16),
            shape((1, half), jnp.int32),
        ],
        scratch=[
            pltpu.VMEM((8, half), f32),
            pltpu.VMEM((per, shard_rows), bf16),
            pltpu.VMEM((half, TAIL), bf16),
            pltpu.VMEM((N_BLK * WIDE, dim), f32),
        ],
        scalars=1,
        count=len(second) + 4,
        flops=2 * product,
        moved=4 * shard_rows * dim,
    )(blk, *second, stat_a, left_a, normed, stored_documents)

    got = exchange(sub_terms.reshape(N_GRP * N_BLK, WIDE, LANES), ("grp", "blk"))
    for steps in ([(0, 1, 0), (0, 0, 1), (0, 1, 1)], [(1, 0, 0), (2, 0, 0), (3, 0, 0)]):
        stats = local(merge_kernel, "merge", shape((8, cols), f32), count=4)(
            stats, *[send(stats, *step) for step in steps]
        )
    loss_row, whole, own, other = passage_terms(
        grp, stats, pos_a, pos_b, order, score_a, score_b, query_a, query_b
    )
    losses = loss_row[0, :ROWS]
    got = got.reshape(N_GRP, N_BLK, WIDE, LANES)
    cot = local(cotangent_kernel, "cotangents", shape((N_BLK, N_GRP * SUB, part), bf16), count=1)(got)
    cot, whole, other = lax.optimization_barrier((cot, whole, other))
    other = send_x(other)
    whole = y_sum(whole)
    cot = exchange(cot, "blk")

    values = local(
        act_kernel,
        "act",
        shape((N_GRP, 3 * per, units + part // N_GRP), bf16),
        scratch=[pltpu.VMEM((N_GRP * per, part), f32)],
        scalars=1,
        count=5,
    )(blk, cot, got, down_weight.T, gate_weight, up_weight)
    grads, cotangent = local(
        swiglu_kernel,
        "swiglu",
        [shape((N_GRP, 2 * per, units), bf16), shape((SUB, dim), f32)],
        count=1,
    )(exchange(values, "grp"))
    grads, other = lax.optimization_barrier((grads, other))
    rest = local(x_sum_kernel, "x_sum", shape(own.shape, bf16), count=2)(own, other)
    grads, rest = lax.optimization_barrier((grads, rest))
    rest = y_sum(rest)
    normed_part = local(backward_kernel, "backward", shape((N_GRP, per, part), bf16), count=3)(
        exchange(grads, "grp"), gate_weight, up_weight
    )
    normed_part, whole = lax.optimization_barrier((normed_part, whole))
    own, other = local(
        x_split_kernel, "x_split", [shape((shard_rows // N_GRP, Y_FIRST), bf16)] * 2, scalars=1, count=1
    )(grp, whole)
    normed_part, other = lax.optimization_barrier((normed_part, other))
    other = send_x(other)
    back = exchange(normed_part.reshape(N_GRP * N_BLK, SUB, part), ("grp", "blk"))
    passage_grads = local(passage_kernel, "passages", shape((shard_rows // N_GRP, dim), f32), count=3)(
        own, other, rest
    )
    hidden_grads = local(hidden_kernel, "hidden", shape((SUB, dim), f32), count=4)(
        back.reshape(N_GRP, N_BLK, SUB, part), cotangent, last_hidden, gain
    )
    return (losses, passage_grads, hidden_grads)


def solution(mesh):
    return jax.shard_map(
        shards,
        mesh=mesh,
        in_specs=(
            P(("blk", "grp"), None),
            P("blk", None),
            P(("blk", "grp")),
            P(("blk", "grp"), None),
            P(),
            P("grp", "blk"),
            P("grp", "blk"),
            P("blk", "grp"),
        ),
        out_specs=(P(("blk", "grp")), P(("blk", "grp"), None), P(("blk", "grp"), None)),
        check_vma=False,
    )
```

```python
import functools

import jax
import jax.numpy as jnp
from jax import lax
from jax.experimental import pallas as pl
from jax.experimental.pallas import tpu as pltpu
from jax.sharding import PartitionSpec as P

sharpness_scale = 20.0
epsilon = 1e-06
contract_last = (((1,), (1,)), ((), ()))
Z, X, C = 4, 2, 2
N_BLK, N_GRP = 16, 8
POS_BASE = 128
TAIL = 128
ROWS = 32
SUB = 2
WIDE = 3 * SUB
LANES = 512
Y_FIRST = 2560
GX, GY = 2, 4
Y_GROUPS = [[x * GY + y for y in range(GY)] for x in range(GX)]
TILE = 256
f32, bf16 = jnp.float32, jnp.bfloat16
VMEM = pl.BlockSpec(memory_space=pltpu.VMEM)
SMEM = pl.BlockSpec(memory_space=pltpu.SMEM)


def local(kernel, name, out_shape, scratch=(), scalars=0, count=0, flops=0, moved=0, vmem=32):
    return pl.pallas_call(
        kernel,
        in_specs=[SMEM] * scalars + [VMEM] * count,
        out_specs=jax.tree.map(lambda _: VMEM, out_shape),
        out_shape=out_shape,
        scratch_shapes=list(scratch),
        compiler_params=pltpu.CompilerParams(vmem_limit_bytes=vmem * 1024 * 1024),
        cost_estimate=pl.CostEstimate(flops=flops, bytes_accessed=moved, transcendentals=0),
        name=name,
    )


def blk_shift(dz, dx, dc):
    pairs = []
    for s in range(N_BLK):
        z, x, c = s // (X * C), s // C % X, s % C
        pairs.append((s, ((z + dz) % Z * X + (x + dx) % X) * C + (c + dc) % C))
    return pairs


def send(v, *shift):
    return lax.ppermute(v, "blk", blk_shift(*shift))


def near_column(block):
    own = [block, send(block, 1, 0, 0), send(block, -1, 0, 0), send(block, 0, 1, 0)]
    return own + [send(v, 0, 0, 1) for v in own]


def far_column(below, above, across):
    across_below = send(across, 1, 0, 0)
    far = send(above, -1, 0, 0)
    across_above = send(above, 0, 1, 0)
    return across_below, far, across_above


def far_rest(across_below, far, across_above, half):
    own = [
        across_below,
        far,
        across_above,
        send(across_below[:half], 1, 0, 0),
        send(far[half:], 0, 1, 0),
    ]
    return own + [send(v, 0, 0, 1) for v in own]


def places_of(blk):
    z, x, c = blk // (X * C), blk // C % X, blk % C
    shifts = [(0, 0), (-1, 0), (1, 0), (0, 1)], [(-1, 1), (2, 0), (1, 1), (2, 1)]
    return [
        ((z + dz + Z) % Z * X + (x + dx) % X) * C + (c + dc) % C
        for batch in shifts
        for dc in range(C)
        for dz, dx in batch
    ]


def block_kernel(pos_ref, query_ref, out_ref):
    dim = query_ref.shape[1]
    out_ref[:, :dim] = query_ref[...]
    line = lax.broadcasted_iota(jnp.int32, (ROWS, TAIL), 0)
    lane = lax.broadcasted_iota(jnp.int32, (ROWS, TAIL), 1)
    index = jnp.zeros_like(line)
    for r in range(ROWS):
        index = jnp.where(line == r, pos_ref[r], index)
    coded = jnp.where(lane == 0, index // POS_BASE, jnp.where(lane == 1, index % POS_BASE, 0))
    out_ref[:, dim:] = coded.astype(f32).astype(bf16)


def split3(v):
    hi = v.astype(bf16)
    rest = v - hi.astype(f32)
    mid = rest.astype(bf16)
    return hi, mid, (rest - mid.astype(f32)).astype(bf16)


def exact_dot(v, onehot, dims):
    parts = [lax.dot_general(p, onehot, dims, preferred_element_type=f32) for p in split3(v)]
    return parts[0] + parts[1] + parts[2]


def batch_scores(first_slot, blocks, doc_ref, score_ref, query_ref, stat_ref, pos_ref, left_ref, tail_ref):
    half, dim = query_ref.shape
    at = 0
    for block in blocks:
        rows = block.shape[0]
        query_ref[at : at + rows, :] = block[:, :dim]
        tail_ref[at : at + rows, :] = block[:, dim:]
        at += rows
    lane = lax.broadcasted_iota(jnp.int32, (8, TAIL), 1)
    line = lax.broadcasted_iota(jnp.int32, (8, TAIL), 0)
    pick = jnp.where(lane == line, 1.0, 0.0).astype(bf16)
    parts = lax.dot_general(pick, tail_ref[...], contract_last, preferred_element_type=f32)
    positive = (parts[0:1] * POS_BASE + parts[1:2]).astype(jnp.int32) - first_slot
    pos_ref[...] = positive
    steps = doc_ref.shape[0] // TILE

    def multiply(t, top):
        at = pl.multiple_of(t * TILE, TILE)
        scores = sharpness_scale * lax.dot_general(
            doc_ref[pl.ds(at, TILE), :], query_ref[...], contract_last, preferred_element_type=f32
        )
        score_ref[pl.ds(at, TILE), :] = scores
        return jnp.maximum(top, jnp.max(scores, axis=0, keepdims=True))

    top = lax.fori_loop(0, steps, multiply, jnp.full((1, half), -jnp.inf, f32))
    wide = 2 * SUB
    lines = half // ROWS * wide
    line = lax.broadcasted_iota(jnp.int32, (lines, half), 0)
    lane = lax.broadcasted_iota(jnp.int32, (lines, half), 1)
    wanted = jnp.where(lane == line // wide * ROWS + line % SUB, 1.0, 0.0).astype(bf16)
    is_u = lax.broadcasted_iota(jnp.int32, (lines, TILE), 0) % wide < SUB

    def sums(t, carry):
        at = pl.multiple_of(t * TILE, TILE)
        scores = score_ref[pl.ds(at, TILE), :]
        hit = at + lax.broadcasted_iota(jnp.int32, scores.shape, 0) == positive
        exps = jnp.exp(scores - top)
        total = carry[0] + jnp.sum(exps, axis=0, keepdims=True)
        found = carry[1] + jnp.sum(jnp.where(hit, scores, 0.0), axis=0, keepdims=True)
        others = jnp.where(hit, 0.0, exps).astype(bf16)
        onehot = jnp.where(hit, 1.0, 0.0).astype(bf16)
        left_ref[:, pl.ds(at, TILE)] = jnp.where(
            is_u,
            lax.dot_general(wanted, others, contract_last, preferred_element_type=f32),
            lax.dot_general(wanted, onehot, contract_last, preferred_element_type=f32),
        ).astype(bf16)
        return total, found

    zero = jnp.zeros((1, half), f32)
    total, found = lax.fori_loop(0, steps, sums, (zero, zero))
    stat_ref[...] = jnp.concatenate([top, total, found, jnp.zeros((5, half), f32)], axis=0)


def first_kernel(blk_ref, *refs):
    blocks, refs = refs[:-10], refs[-10:]
    hidden_ref, gain_ref, doc_ref, normed_ref = refs[:4]
    hidden = hidden_ref[...].astype(f32)
    inv_rms = lax.rsqrt(jnp.mean(hidden * hidden, axis=1, keepdims=True) + epsilon)
    normed = hidden * inv_rms * gain_ref[...]
    normed_ref[...] = jnp.concatenate([normed, jnp.zeros((8 - SUB, hidden.shape[1]), f32)], axis=0).astype(bf16)
    batch_scores(blk_ref[0] * doc_ref.shape[0], blocks, doc_ref, *refs[4:])


def second_kernel(blk_ref, *refs):
    blocks, refs = refs[:-14], refs[-14:]
    stat_first, left_first, normed_ref, doc_ref, all_ref, sub_ref, order_ref = refs[:7]
    score_ref, query_ref, pos_ref, stat_ref, left_ref, tail_ref, acc = refs[7:]
    cols = order_ref.shape[0]
    lane = lax.broadcasted_iota(jnp.int32, (ROWS, cols), 1)
    line = lax.broadcasted_iota(jnp.int32, (ROWS, cols), 0)
    places = places_of(blk_ref[0])
    for k in range(N_BLK):
        order_ref[k * ROWS : (k + 1) * ROWS, :] = jnp.where(lane == places[k] * ROWS + line, 1.0, 0.0).astype(bf16)
    batch_scores(
        blk_ref[0] * doc_ref.shape[0], blocks, doc_ref, score_ref, query_ref, stat_ref, pos_ref, left_ref, tail_ref
    )
    stats = jnp.concatenate([stat_first[...], stat_ref[...]], axis=1)
    stats = exact_dot(stats, order_ref[...], (((1,), (0,)), ((), ())))
    all_ref[...] = stats
    parts = split3(stats)
    four = 2 * SUB
    lines = N_BLK * WIDE
    line = lax.broadcasted_iota(jnp.int32, (lines, N_BLK * four), 0)
    lane = lax.broadcasted_iota(jnp.int32, (lines, N_BLK * four), 1)
    swap = jnp.zeros(line.shape, f32)
    for k in range(N_BLK):
        swap = jnp.where((lane // four == k) & (line == places[k] * WIDE + lane % four), 1.0, swap)
    left = jnp.concatenate([left_first[...], left_ref[...]], axis=0)
    left = jnp.dot(swap.astype(bf16), left, preferred_element_type=f32).astype(bf16)
    line = lax.broadcasted_iota(jnp.int32, (lines, 8), 0)
    lane = lax.broadcasted_iota(jnp.int32, (lines, 8), 1)
    spread = jnp.where((line % WIDE - four == lane) & (lane < SUB), 1.0, 0.0).astype(bf16)
    acc[...] = jnp.dot(spread, normed_ref[...], preferred_element_type=f32)
    acc[...] += jnp.dot(left, doc_ref[...], preferred_element_type=f32)
    line = lax.broadcasted_iota(jnp.int32, (lines, cols), 0)
    lane = lax.broadcasted_iota(jnp.int32, (lines, cols), 1)
    wanted = jnp.where((lane == line // WIDE * ROWS + line % WIDE) & (line % WIDE < SUB), 1.0, 0.0).astype(bf16)
    stat_rows = [
        lax.dot_general(wanted, p, contract_last, preferred_element_type=f32).astype(bf16) for p in parts
    ]
    width = doc_ref.shape[1] // N_GRP
    grads = acc[...].astype(bf16)
    tail = jnp.concatenate(stat_rows + [jnp.zeros((lines, LANES - width - 24), bf16)], axis=1)
    for g in range(N_GRP):
        sub_ref[g] = jnp.concatenate([grads[:, g * width : (g + 1) * width], tail], axis=1)


def merge_kernel(*refs):
    refs, out_ref = refs[:-1], refs[-1]
    top = functools.reduce(jnp.maximum, [r[0:1] for r in refs])
    total = sum(r[1:2] * jnp.exp(r[0:1] - top) for r in refs)
    found = sum(r[2:3] for r in refs)
    out_ref[...] = jnp.concatenate([top, total, found, jnp.zeros_like(out_ref[3:])], axis=0)


def cotangent_kernel(got_ref, cot_ref):
    width = cot_ref.shape[2]
    rows = got_ref[:, :, : 2 * SUB, :].astype(f32)
    terms, hits, tail = rows[:, :, :SUB, :width], rows[:, :, SUB:, :width], rows[:, :, :SUB, width:]
    stat = lambda k: tail[..., k : k + 1] + tail[..., k + 8 : k + 9] + tail[..., k + 16 : k + 17]
    top = jnp.max(stat(0), axis=1, keepdims=True)
    total = jnp.sum(stat(1) * jnp.exp(stat(0) - top), axis=1, keepdims=True)
    log_total = top + jnp.log(total)
    found = jnp.sum(stat(2), axis=1, keepdims=True)
    scale = jnp.exp(stat(0) - log_total)
    grads = jnp.sum(scale * terms + (jnp.exp(found - log_total) - 1.0) * hits, axis=1)
    grads = sharpness_scale * grads
    grads = jnp.concatenate([grads[g] for g in range(N_GRP)], axis=0).astype(bf16)
    for b in range(N_BLK):
        cot_ref[b] = grads


def weight_kernel(grp_ref, stats_ref, pos_a, pos_b, order_ref, first_ref, second_ref, query_a, query_b, *refs):
    loss_ref, whole_ref, own_ref, other_ref, total = refs
    step = pl.program_id(0)
    cols = order_ref.shape[1]
    half = cols // 2

    @pl.when(step == 0)
    def _():
        log_total = stats_ref[0:1] + jnp.log(stats_ref[1:2])
        losses = log_total - stats_ref[2:3]
        both = jnp.concatenate([log_total, losses, jnp.zeros((6, cols), f32)], axis=0)
        both = exact_dot(both, order_ref[...], contract_last)
        loss_ref[...] = both[1:2]
        total[...] = both[0:1]

    rows = first_ref.shape[2]
    out = None
    for k, (score_ref, query_ref, pos_ref) in enumerate(
        ((first_ref, query_a, pos_a), (second_ref, query_b, pos_b))
    ):
        scores = score_ref[...].reshape(GX * rows, half)
        line = lax.broadcasted_iota(jnp.int32, scores.shape, 0)
        slot = (line // rows * GY + step) * rows + line % rows
        onehot = jnp.where(slot == pos_ref[...], 1.0, 0.0)
        weights = (jnp.exp(scores - total[:, k * half : (k + 1) * half]) - onehot).astype(bf16)
        term = jnp.dot(weights, query_ref[...], preferred_element_type=f32)
        out = term if out is None else out + term
    out = sharpness_scale * out
    first_x = grp_ref[0] // GY == 0
    whole_ref[...] = out[:, :Y_FIRST].astype(bf16)
    own_ref[...] = jnp.where(first_x, out[:rows, Y_FIRST:], out[rows:, Y_FIRST:]).astype(bf16)
    other_ref[...] = jnp.where(first_x, out[rows:, Y_FIRST:], out[:rows, Y_FIRST:]).astype(bf16)


def passage_terms(grp, stats, pos_a, pos_b, order, score_a, score_b, query_a, query_b):
    shard_rows, half = score_a.shape
    dim = query_a.shape[1]
    rows = shard_rows // N_GRP
    shape = jax.ShapeDtypeStruct
    fixed = lambda v: pl.BlockSpec(v.shape, lambda i: (0,) * len(v.shape))
    scores = pl.BlockSpec((GX, 1, rows, half), lambda i: (0, i, 0, 0))
    apart = pl.BlockSpec((rows, dim - Y_FIRST), lambda i: (i, 0))
    loss = shape((1, 2 * half), f32)
    return pl.pallas_call(
        weight_kernel,
        grid=(GY,),
        in_specs=[SMEM, fixed(stats), fixed(pos_a), fixed(pos_b), fixed(order), scores, scores]
        + [fixed(query_a), fixed(query_b)],
        out_specs=[fixed(loss), pl.BlockSpec((GX * rows, Y_FIRST), lambda i: (i, 0)), apart, apart],
        out_shape=[loss, shape((shard_rows, Y_FIRST), bf16)]
        + [shape((GY * rows, dim - Y_FIRST), bf16)] * 2,
        scratch_shapes=[pltpu.VMEM((1, 2 * half), f32)],
        compiler_params=pltpu.CompilerParams(vmem_limit_bytes=52 * 1024 * 1024),
        cost_estimate=pl.CostEstimate(
            flops=4 * shard_rows * half * dim, bytes_accessed=4 * shard_rows * dim, transcendentals=0
        ),
        name="passage_terms",
    )(
        grp,
        stats,
        pos_a,
        pos_b,
        order,
        score_a.reshape(GX, GY, rows, half),
        score_b.reshape(GX, GY, rows, half),
        query_a,
        query_b,
    )


def x_sum_kernel(own_ref, got_ref, out_ref):
    out_ref[...] = (own_ref[...].astype(f32) + got_ref[...].astype(f32)).astype(bf16)


def x_split_kernel(grp_ref, both_ref, own_ref, other_ref):
    rows = own_ref.shape[0]
    first_x = grp_ref[0] // GY == 0
    above, below = both_ref[:rows].astype(f32), both_ref[rows:].astype(f32)
    own_ref[...] = jnp.where(first_x, above, below).astype(bf16)
    other_ref[...] = jnp.where(first_x, below, above).astype(bf16)


def passage_kernel(own_ref, got_ref, rest_ref, out_ref):
    out_ref[:, :Y_FIRST] = own_ref[...].astype(f32) + got_ref[...].astype(f32)
    out_ref[:, Y_FIRST:] = rest_ref[...].astype(f32)


def send_x(v):
    return lax.ppermute(v, "grp", [(g, (g + GY) % N_GRP) for g in range(N_GRP)])


def y_sum(v):
    return lax.psum_scatter(v, "grp", scatter_dimension=0, axis_index_groups=Y_GROUPS, tiled=True)


def act_kernel(blk_ref, cot_ref, got_ref, down_ref, gate_ref, up_ref, out_ref, normed):
    part, units = down_ref.shape
    for g in range(N_GRP):
        for b in range(N_BLK):
            at = (g * N_BLK + b) * SUB
            normed[at : at + SUB, :] = got_ref[g, b, 2 * SUB :, :part].astype(f32)
    rows = cot_ref[...].reshape(-1, part)
    count = rows.shape[0]
    line = lax.broadcasted_iota(jnp.int32, (count, count), 0)
    lane = lax.broadcasted_iota(jnp.int32, (count, count), 1)
    per = N_BLK * SUB
    swap = jnp.where(lane == (line % per // SUB * N_GRP + line // per) * SUB + line % SUB, 1.0, 0.0).astype(bf16)
    rows = jnp.dot(swap, rows, preferred_element_type=f32).astype(bf16)
    values = [jnp.dot(rows, down_ref[...], preferred_element_type=f32).astype(bf16)]
    rows = normed[...].astype(bf16)
    values.append(jnp.dot(rows, gate_ref[...], preferred_element_type=f32).astype(bf16))
    values.append(jnp.dot(rows, up_ref[...], preferred_element_type=f32).astype(bf16))
    own = cot_ref[blk_ref[0]]
    width = part // N_GRP
    blank = jnp.zeros((per - N_GRP * SUB, width), bf16)
    for g in range(N_GRP):
        mine = own[g * SUB : (g + 1) * SUB].astype(f32)
        pieces = [mine[:, k * width : (k + 1) * width] for k in range(N_GRP)]
        pieces = jnp.concatenate(pieces, axis=0).astype(bf16)
        for k in range(3):
            out_ref[g, k * per : (k + 1) * per, :units] = values[k][g * per : (g + 1) * per]
        out_ref[g, :per, units : units + width] = jnp.concatenate([pieces, blank], axis=0)
        out_ref[g, per:, units : units + width] = jnp.zeros((2 * per, width), bf16)


def swiglu_kernel(got_ref, out_ref, cot_ref):
    per = got_ref.shape[1] // 3
    units = out_ref.shape[2]
    sums = jnp.sum(got_ref[:, :, :units].astype(f32), axis=0)
    act_grad, gate_value, up_value = sums[:per], sums[per : 2 * per], sums[2 * per :]
    gate_sigmoid = jax.nn.sigmoid(gate_value)
    up_grad = (act_grad * gate_value * gate_sigmoid).astype(bf16)
    gate_grad = (act_grad * up_value * gate_sigmoid * (1.0 + gate_value * (1.0 - gate_sigmoid))).astype(bf16)
    for g in range(N_GRP):
        out_ref[g, :per] = gate_grad
        out_ref[g, per:] = up_grad
    pieces = got_ref[:, : N_GRP * SUB, units:].astype(f32)
    cot_ref[...] = jnp.concatenate(
        [pieces[g, k * SUB : (k + 1) * SUB] for g in range(N_GRP) for k in range(N_GRP)], axis=1
    )


def backward_kernel(grad_ref, gate_ref, up_ref, out_ref):
    per = grad_ref.shape[1] // 2
    both = grad_ref[...]
    gate_grad = both[:, :per].reshape(N_GRP * per, -1)
    up_grad = both[:, per:].reshape(N_GRP * per, -1)
    total = lax.dot_general(gate_grad, gate_ref[...], contract_last, preferred_element_type=f32)
    total += lax.dot_general(up_grad, up_ref[...], contract_last, preferred_element_type=f32)
    for g in range(N_GRP):
        out_ref[g] = total[g * per : (g + 1) * per].astype(bf16)


def hidden_kernel(back_ref, cot_ref, hidden_ref, gain_ref, out_ref):
    sums = jnp.sum(back_ref[...].astype(f32), axis=1)
    normed_grad = jnp.concatenate([sums[g] for g in range(N_GRP)], axis=1)
    hidden = hidden_ref[...].astype(f32)
    inv_rms = lax.rsqrt(jnp.mean(hidden * hidden, axis=1, keepdims=True) + epsilon)
    scaled = normed_grad * gain_ref[...]
    mean = jnp.mean(hidden * scaled, axis=1, keepdims=True)
    out_ref[...] = cot_ref[...] + inv_rms * scaled - hidden * inv_rms * inv_rms * inv_rms * mean


def exchange(v, axis):
    return lax.all_to_all(v, axis, 0, 0, tiled=True)


def shards(
    queries, stored_documents, positive, last_hidden, norm_gain, gate_weight, up_weight, down_weight
):
    shape = jax.ShapeDtypeStruct
    blk = lax.axis_index("blk").astype(jnp.int32)[None]
    grp = lax.axis_index("grp").astype(jnp.int32)[None]
    shard_rows, dim = stored_documents.shape
    part = dim // N_GRP
    units = gate_weight.shape[1]
    cols = N_BLK * ROWS
    half = cols // 2
    per = N_BLK * SUB
    gain = norm_gain[None]

    block = local(block_kernel, "block", shape((ROWS, dim + TAIL), bf16), scalars=1, count=1)(
        positive, queries
    )
    first = near_column(block)
    second = far_column(*first[1:4])

    product = 2 * shard_rows * half * dim
    normed, score_a, query_a, stat_a, pos_a, left_a = local(
        first_kernel,
        "first_scores",
        [
            shape((8, dim), bf16),
            shape((shard_rows, half), f32),
            shape((half, dim), bf16),
            shape((8, half), f32),
            shape((1, half), jnp.int32),
            shape((per, shard_rows), bf16),
        ],
        scratch=[pltpu.VMEM((half, TAIL), bf16)],
        scalars=1,
        count=len(first) + 3,
        flops=2 * product,
        moved=4 * shard_rows * dim,
    )(blk, *first, last_hidden, gain, stored_documents)
    second, left_a = lax.optimization_barrier((second, left_a))
    second = far_rest(*second, ROWS // 2)
    stats, sub_terms, order, score_b, query_b, pos_b = local(
        second_kernel,
        "second_scores",
        [
            shape((8, cols), f32),
            shape((N_GRP, N_BLK * WIDE, LANES), bf16),
            shape((cols, cols), bf16),
            shape((shard_rows, half), f32),
            shape((half, dim), bf16),
            shape((1, half), jnp.int32),
        ],
        scratch=[
            pltpu.VMEM((8, half), f32),
            pltpu.VMEM((per, shard_rows), bf16),
            pltpu.VMEM((half, TAIL), bf16),
            pltpu.VMEM((N_BLK * WIDE, dim), f32),
        ],
        scalars=1,
        count=len(second) + 4,
        flops=2 * product,
        moved=4 * shard_rows * dim,
    )(blk, *second, stat_a, left_a, normed, stored_documents)

    got = exchange(sub_terms.reshape(N_GRP * N_BLK, WIDE, LANES), ("grp", "blk"))
    for steps in ([(0, 1, 0), (0, 0, 1), (0, 1, 1)], [(1, 0, 0), (2, 0, 0), (3, 0, 0)]):
        stats = local(merge_kernel, "merge", shape((8, cols), f32), count=4)(
            stats, *[send(stats, *step) for step in steps]
        )
    loss_row, whole, own, other = passage_terms(
        grp, stats, pos_a, pos_b, order, score_a, score_b, query_a, query_b
    )
    losses = loss_row[0, :ROWS]
    got = got.reshape(N_GRP, N_BLK, WIDE, LANES)
    cot = local(cotangent_kernel, "cotangents", shape((N_BLK, N_GRP * SUB, part), bf16), count=1)(got)
    cot, whole, other = lax.optimization_barrier((cot, whole, other))
    other = send_x(other)
    whole = y_sum(whole)
    cot = exchange(cot, "blk")

    values = local(
        act_kernel,
        "act",
        shape((N_GRP, 3 * per, units + part // N_GRP), bf16),
        scratch=[pltpu.VMEM((N_GRP * per, part), f32)],
        scalars=1,
        count=5,
    )(blk, cot, got, down_weight.T, gate_weight, up_weight)
    grads, cotangent = local(
        swiglu_kernel,
        "swiglu",
        [shape((N_GRP, 2 * per, units), bf16), shape((SUB, dim), f32)],
        count=1,
    )(exchange(values, "grp"))
    grads, other = lax.optimization_barrier((grads, other))
    rest = local(x_sum_kernel, "x_sum", shape(own.shape, bf16), count=2)(own, other)
    grads, rest = lax.optimization_barrier((grads, rest))
    rest = y_sum(rest)
    normed_part = local(backward_kernel, "backward", shape((N_GRP, per, part), bf16), count=3)(
        exchange(grads, "grp"), gate_weight, up_weight
    )
    normed_part, whole = lax.optimization_barrier((normed_part, whole))
    own, other = local(
        x_split_kernel, "x_split", [shape((shard_rows // N_GRP, Y_FIRST), bf16)] * 2, scalars=1, count=1
    )(grp, whole)
    normed_part, other = lax.optimization_barrier((normed_part, other))
    other = send_x(other)
    back = exchange(normed_part.reshape(N_GRP * N_BLK, SUB, part), ("grp", "blk"))
    passage_grads = local(passage_kernel, "passages", shape((shard_rows // N_GRP, dim), f32), count=3)(
        own, other, rest
    )
    hidden_grads = local(hidden_kernel, "hidden", shape((SUB, dim), f32), count=4)(
        back.reshape(N_GRP, N_BLK, SUB, part), cotangent, last_hidden, gain
    )
    return (losses, passage_grads, hidden_grads)


def solution(mesh):
    return jax.shard_map(
        shards,
        mesh=mesh,
        in_specs=(
            P(("blk", "grp"), None),
            P("blk", None),
            P(("blk", "grp")),
            P(("blk", "grp"), None),
            P(),
            P("grp", "blk"),
            P("grp", "blk"),
            P("blk", "grp"),
        ),
        out_specs=(P(("blk", "grp")), P(("blk", "grp"), None), P(("blk", "grp"), None)),
        check_vma=False,
    )
```
